128 devices in a mesh: fsdp: 32 (over z, x, y_hi), expert: 4 (over y_lo, core).
Axes of the slice: x: 4, y: 4 (y_hi: 2, y_lo: 2; y = y_hi * 2 + y_lo), z: 4, core: 2. Of those that a mesh axis runs over, the one named last changes fastest.
Arguments:
- tokens: bfloat16 [4096, 4096], P('fsdp'), may hold values from -6 to 6
- expert_ids: int32 [4096, 8], P('fsdp'), may hold values from 0 to 127, all different within a row; in each aligned block of 128 rows (0 to 127, 128 to 255, ...) at most 12 rows name the same one
- route_weights: float32 [4096, 8], P('fsdp'), may hold values from 0.1 to 1
- d_out: bfloat16 [4096, 4096], P('fsdp'), may hold values from -6 to 6
- gate_weight: bfloat16 [32, 4096, 1536], P('fsdp', None, 'expert'), may hold values from -0.09375 to 0.09375
- up_weight: bfloat16 [32, 4096, 1536], P('fsdp', None, 'expert'), may hold values from -0.09375 to 0.09375
- down_weight: bfloat16 [32, 1536, 4096], P('fsdp', 'expert'), may hold values from -0.15625 to 0.15625
Outputs:
- moe_out: bfloat16 [4096, 4096], P('fsdp')
- d_tokens: bfloat16 [4096, 4096], P('fsdp')
- d_route_weights: float32 [4096, 8], P('fsdp')
- d_gate_weight: bfloat16 [32, 4096, 1536], P('fsdp', None, 'expert')
- d_up_weight: bfloat16 [32, 4096, 1536], P('fsdp', None, 'expert')
- d_down_weight: bfloat16 [32, 1536, 4096], P('fsdp', 'expert')
The draws below stay inside these ranges and needn't reach their ends.
Inputs may be any that keep to these rules, and one draw needn't show every extreme that they name: `expert_ids`: each row names 8 different experts. Among the rows of one block of 128 tokens no expert is named more than 12 times. Experts from 32 on are held elsewhere.
All inputs are finite; a program needn't handle non-finite values.
Results may differ from the reference program's by a relative error of at most 0.0065.
Values may be sent and summed in bfloat16 or wider, within the bound.
A program may use at most 128 MiB of HBM per device.

```python
import math
import jax
import jax.numpy as jnp
import numpy as np
from jax import lax

D = 4096
F = 1536
EXPERTS = 128
TOPK = 8
EXP_DEV = 1
TOK_DEV = 128
CAP = 12
E_WIN = 32
TOKENS = 4096
N_FSDP = 32


def shard_levels(stream_key, extent, pieces, low, largest):
    def one(position, blocks):
        heights = jax.random.uniform(jax.random.fold_in(jax.random.fold_in(stream_key, 6), position), (blocks,), jnp.float32, low / len(pieces), largest / len(pieces))
        return jnp.repeat(jnp.exp(heights), extent[position] // blocks).reshape((-1,) + (1,) * (len(extent) - position - 1))

    factor_of = one(*pieces[0])
    for cut in pieces[1:]:
        factor_of = factor_of * one(*cut)
    return factor_of


def shared_out(rng, own, number, rows, count, top, most, skew):
    sequence = jax.random.permutation(rng, count)
    heavy_load, ordinary = shares(count, rows * top, most, skew, True), shares(count, rows * top, most, skew, False)
    places = jnp.arange(count)

    def named(lengths, offset_by):
        used = int((lengths > 0).sum())
        fixed = max(1, used // 4)
        moved = fixed + (places - fixed + offset_by * (used - fixed)) % max(1, count - fixed)
        return jnp.zeros((count,), jnp.int32).at[sequence[jnp.where(places < fixed, places, moved)]].set(jnp.asarray(lengths, jnp.int32))

    lengths = jnp.where(number % 4 == 0, named(heavy_load, number // 4), named(ordinary, number - number // 4 - 1))
    mixed = jax.random.permutation(jax.random.fold_in(own, 3), count)
    source_of, taker = mixed[0:count // 2 * 2:2], mixed[1:count // 2 * 2:2]
    room = jnp.minimum(lengths[source_of] - 1, most - lengths[taker]) // 2
    room = jnp.where((source_of == sequence[0]) | (taker == sequence[0]) | (lengths[taker] == 0), 0, jnp.maximum(room, 0))
    moved = jax.random.randint(jax.random.fold_in(own, 4), (count // 2,), 0, 1 << 20) % (room + 1)
    lengths = lengths.at[source_of].add(-moved).at[taker].add(moved)
    members = jnp.searchsorted(jnp.cumsum(lengths), jnp.arange(rows * top), side="right").astype(jnp.int32)
    table = members.reshape(top, rows).T
    table = table[jax.random.permutation(jax.random.fold_in(own, 1), rows)]
    offset_by = jax.random.randint(jax.random.fold_in(own, 2), (rows, 1), 0, top)
    return jnp.take_along_axis(table, (jnp.arange(top)[None, :] + offset_by) % top, axis=1)


def shares(number_of, total, most, lean, full):
    portions = [(1 << 20) // math.isqrt(grade ** lean) + 1 for grade in range(1, number_of + 1)]
    largest = most if full else min(most, max(-(-total // number_of), total * portions[0] // sum(portions)))
    least = 1 if total - largest >= number_of - 1 else 0
    given, rest = [largest] + [least] * (number_of - 1), total - largest - least * (number_of - 1)
    while rest > 0:
        free = [i for i in range(1, number_of) if given[i] < largest] or [i for i in range(1, number_of) if given[i] < most]
        whole, remaining = sum([portions[i] for i in free]), rest
        for i in free:
            extra = min(most - given[i], max(1, remaining * portions[i] // whole), rest)
            given[i] = given[i] + extra
            rest = rest - extra
    return np.array(given)


def gaussian(own_key, shape, scale, most, shards=(), kind=jnp.bfloat16):
    level = shard_levels(own_key, shape, shards, -0.22, 0.18) if shards else 1.0
    drawn = jax.random.normal(own_key, shape, jnp.float32) * scale * level
    return jnp.minimum(jnp.maximum(drawn, -most), most).astype(kind)


def setup_inputs(seed: int = 0) -> dict:
    splits = jax.random.split(jax.random.key(seed), 8)
    tokens = gaussian(splits[0], (TOKENS, D), 1.0, 6.0, ((0, 32),))
    expert_ids_keys = jax.random.split(jax.random.fold_in(splits[1], 1), TOKENS // TOK_DEV)
    expert_ids_turns = jax.random.permutation(jax.random.fold_in(splits[1], 3), TOKENS // TOK_DEV)
    expert_ids = jax.vmap(lambda own, number: shared_out(jax.random.fold_in(splits[1], 2), own, number, TOK_DEV, EXPERTS, TOPK, CAP, 0))(expert_ids_keys, expert_ids_turns).reshape((TOKENS, TOPK))
    route_weights = jnp.clip(0.1 + 0.9 * jax.random.uniform(splits[2], (TOKENS, TOPK), jnp.float32) ** shard_levels(splits[2], (TOKENS, TOPK), ((0, 32),), -0.2, 0.2), 0.1, 1.0)
    d_out = gaussian(splits[3], (TOKENS, D), 1.0, 6.0, ((0, 32),))
    gate_weight = gaussian(splits[4], (E_WIN, D, F), D ** -0.5, 0.09375, ((0, 32), (2, 4)))
    up_weight = gaussian(splits[5], (E_WIN, D, F), D ** -0.5, 0.09375, ((0, 32), (2, 4)))
    down_weight = gaussian(splits[6], (E_WIN, F, D), F ** -0.5, 0.15625, ((0, 32), (1, 4)))
    return dict(tokens=tokens, expert_ids=expert_ids, route_weights=route_weights, d_out=d_out, gate_weight=gate_weight, up_weight=up_weight, down_weight=down_weight)


def slot_table(route_ids, n_win, capacity):
    total_rows = route_ids.shape[0] * route_ids.shape[1]
    flat_ids = route_ids.reshape(total_rows)
    labels = jnp.arange(n_win, dtype=jnp.int32)
    onehot = (flat_ids[:, None] == labels[None, :]).astype(jnp.int32)
    rank_all = jnp.sum((jnp.cumsum(onehot, axis=0) - 1) * onehot, axis=1).astype(jnp.int32)
    inside = flat_ids < n_win
    slot_of = jnp.where(inside, flat_ids * capacity + rank_all, n_win * capacity).astype(jnp.int32)
    orders = jnp.arange(total_rows, dtype=jnp.int32)
    assign = jnp.zeros((n_win * capacity,), jnp.int32).at[slot_of].set(orders, mode="drop")
    filled = jnp.zeros((n_win * capacity,), jnp.float32).at[slot_of].set(1.0, mode="drop")
    return slot_of, assign, filled


def rounded(value):
    return lax.optimization_barrier(value.astype(jnp.bfloat16)).astype(jnp.float32)


def expert_pass(packed):
    rows_in, cot_rows, w_gate, w_up, w_down = packed
    rows_in = rows_in.astype(jnp.float32)
    cot_rows = cot_rows.astype(jnp.float32)
    w_gate = w_gate.astype(jnp.float32)
    w_up = w_up.astype(jnp.float32)
    w_down = w_down.astype(jnp.float32)
    gate_pre = jnp.dot(rows_in, w_gate)
    up_pre = jnp.dot(rows_in, w_up)
    sigma = jax.nn.sigmoid(gate_pre)
    active = gate_pre * sigma
    hidden = rounded(active * up_pre)
    out_rows = jnp.dot(hidden, w_down).astype(jnp.bfloat16)
    d_hidden = jnp.dot(cot_rows, w_down.T)
    slope = sigma * (1.0 + gate_pre * (1.0 - sigma))
    d_gate = rounded(d_hidden * up_pre * slope)
    d_up = rounded(d_hidden * active)
    dx_rows = (jnp.dot(d_gate, w_gate.T) + jnp.dot(d_up, w_up.T)).astype(jnp.bfloat16)
    grad_gate = jnp.dot(rows_in.T, d_gate).astype(jnp.bfloat16)
    grad_up = jnp.dot(rows_in.T, d_up).astype(jnp.bfloat16)
    grad_down = jnp.dot(hidden.T, cot_rows).astype(jnp.bfloat16)
    return out_rows, dx_rows, grad_gate, grad_up, grad_down


def gather_back(packed):
    ret_out, ret_dx, slot_of, weights, cot_block = packed
    n_slots = ret_out.shape[0]
    mask = (slot_of < n_slots).astype(jnp.float32)[:, None]
    index = jnp.minimum(slot_of, n_slots - 1)
    out_rows = ret_out[index].astype(jnp.float32) * mask
    dx_rows = ret_dx[index].astype(jnp.float32) * mask
    tok_rows, top = weights.shape
    moe_out = jnp.sum((out_rows * weights.reshape(-1)[:, None]).reshape(tok_rows, top, -1), axis=1).astype(jnp.bfloat16)
    d_tokens = jnp.sum(dx_rows.reshape(tok_rows, top, -1), axis=1).astype(jnp.bfloat16)
    d_route = jnp.sum(out_rows.reshape(tok_rows, top, -1) * cot_block.astype(jnp.float32)[:, None, :], axis=2)
    return moe_out, d_tokens, d_route


def reference(tokens, expert_ids, route_weights, d_out, gate_weight, up_weight, down_weight):
    n_win = N_FSDP * EXP_DEV
    block_ids = expert_ids.reshape(N_FSDP, TOK_DEV, TOPK)
    slot_of, assign, filled = jax.vmap(lambda part_ids: slot_table(part_ids, n_win, CAP))(block_ids)
    token_blocks = tokens.reshape(N_FSDP, TOK_DEV, D)
    cot_blocks = d_out.reshape(N_FSDP, TOK_DEV, D)
    weight_blocks = route_weights.reshape(N_FSDP, TOK_DEV, TOPK)
    source = assign // TOPK
    picker = jax.vmap(lambda block, rows: block[rows])
    rows_in = (picker(token_blocks, source).astype(jnp.float32) * filled[..., None]).astype(jnp.bfloat16)
    scales = jnp.take_along_axis(weight_blocks.reshape(N_FSDP, TOK_DEV * TOPK), assign, axis=1) * filled
    cot_rows = (picker(cot_blocks, source).astype(jnp.float32) * scales[..., None]).astype(jnp.bfloat16)
    per_expert_x = rows_in.reshape(N_FSDP, n_win, CAP, D).transpose(1, 0, 2, 3).reshape(n_win, N_FSDP * CAP, D)
    per_expert_g = cot_rows.reshape(N_FSDP, n_win, CAP, D).transpose(1, 0, 2, 3).reshape(n_win, N_FSDP * CAP, D)
    out_rows, dx_rows, grad_gate, grad_up, grad_down = lax.map(
        expert_pass, (per_expert_x, per_expert_g, gate_weight, up_weight, down_weight))
    back_out = out_rows.reshape(n_win, N_FSDP, CAP, D).transpose(1, 0, 2, 3).reshape(N_FSDP, n_win * CAP, D)
    back_dx = dx_rows.reshape(n_win, N_FSDP, CAP, D).transpose(1, 0, 2, 3).reshape(N_FSDP, n_win * CAP, D)
    moe_out, d_tokens, d_route = lax.map(gather_back, (back_out, back_dx, slot_of, weight_blocks, cot_blocks))
    return (moe_out.reshape(TOKENS, D), d_tokens.reshape(TOKENS, D), d_route.reshape(TOKENS, TOPK),
            grad_gate, grad_up, grad_down)
```

```python
import jax
import jax.numpy as jnp
from jax import lax
from jax.experimental import pallas as pl
from jax.experimental.pallas import tpu as pltpu
from jax.sharding import PartitionSpec as P

MESH = pl.DeviceIdType.MESH
BF = jnp.bfloat16
F32 = jnp.float32

D = 4096
FH = 384
SRC = 32
TOK = 128
CAP = 12
ROWS = SRC * CAP
W = 512
MSG = 4 * CAP
Q = W // 4
HALF = D // 2
NP = HALF // W


def dot(a, b):
    return lax.dot_general(a, b, (((1,), (0,)), ((), ())), preferred_element_type=F32)


def dot_nt(a, b):
    return lax.dot_general(a, b, (((1,), (1,)), ((), ())), preferred_element_type=F32)


def dot_tn(a, b):
    return lax.dot_general(a, b, (((0,), (0,)), ((), ())), preferred_element_type=F32)


def iota(shape, dim):
    return lax.broadcasted_iota(jnp.int32, shape, dim)


def part_and_rank(m):
    part = (
        (m >= CAP).astype(jnp.int32)
        + (m >= 2 * CAP).astype(jnp.int32)
        + (m >= 3 * CAP).astype(jnp.int32)
    )
    return part, m - CAP * part


def over_msg(j):
    return (j * 1366) >> 16


def spread(i, f):
    a, b, c = i % 4, (i // 4) % 4, i // 16
    dz, dx, dy = a, (a + b) % 4, (a + b + c) % 2
    z, x, y = f // 8, (f // 2) % 4, f % 2
    return ((z + dz) % 4) * 8 + ((x + dx) % 4) * 2 + (y + dy) % 2


def wait_bytes(ref, sem):
    pltpu.make_async_copy(ref, ref, sem).wait()


def kernel(
    ids_ref, w_ref, tok_hbm, dout_hbm, gate_hbm, up_hbm, down_hbm,
    moe_hbm, dtok_hbm, droute_ref, dgate_hbm, dup_hbm, ddown_hbm,
    tok_v, dout_v, code_s, wt_s, e_s, gs_s, et_s, whi_s, wlo_s, rhs_s, pm_s,
    s_s, r_s, xg_s, gu_s, dn_s, gu_acc, dh_acc, hid_s, dgu_s,
    xo_s, xi_s, v_s, sr_s, rr_s, acc_s, dq_s, mq_s, dr_s,
    tok_sem, w_sem, ssem, rsem, lsem, fs_sem, fr_sem,
    xs_sem, xr_sem, s2_sem, r2_sem, l2_sem, g_sem,
    ms_sem, mr_sem, ys_sem, yr_sem, hs_sem, hr_sem, ds_sem, dr_sem, o_sem,
):
    f = lax.axis_index("fsdp")
    e = lax.axis_index("expert")
    y, c = e // 2, e % 2
    mate = e + 1 - 2 * c
    other = (e + 2) % 4
    diag = (mate + 2) % 4

    bar = pltpu.get_barrier_semaphore()

    def greet(i, carry):
        f2 = spread(i, f)

        @pl.when(i > 0)
        def _():
            pl.semaphore_signal(bar, inc=1, device_id=(f2, e), device_id_type=MESH)

        pl.semaphore_signal(bar, inc=1, device_id=(f2, other), device_id_type=MESH)
        return carry

    lax.fori_loop(0, SRC, greet, 0)
    pl.semaphore_signal(bar, inc=1, device_id=(f, mate), device_id_type=MESH)
    pl.semaphore_signal(bar, inc=1, device_id=(f, diag), device_id_type=MESH)

    half = pl.ds(pl.multiple_of(c * HALF, HALF), HALF)
    tok_in = pltpu.make_async_copy(tok_hbm.at[:, half], tok_v, tok_sem.at[0])
    dout_in = pltpu.make_async_copy(dout_hbm.at[:, half], dout_v, tok_sem.at[1])
    tok_in.start()
    dout_in.start()
    for j in range(2 * NP):
        cols = pl.ds(j * W, W)
        pltpu.make_async_copy(gate_hbm.at[0, cols, :], gu_s.at[j, :, pl.ds(0, FH)], w_sem.at[0]).start()
        pltpu.make_async_copy(up_hbm.at[0, cols, :], gu_s.at[j, :, pl.ds(FH, FH)], w_sem.at[0]).start()
        pltpu.make_async_copy(down_hbm.at[0, :, cols], dn_s.at[j], w_sem.at[1]).start()

    ids = ids_ref[...]
    wts = w_ref[...]
    lane = iota((TOK, 128), 1)
    named = jnp.zeros((TOK, 128), F32)
    wmat = jnp.zeros((TOK, 128), F32)
    for k in range(ids.shape[1]):
        hit = ids[:, k : k + 1] == lane
        named = named + jnp.where(hit, 1.0, 0.0)
        wmat = wmat + jnp.where(hit, wts[:, k : k + 1], 0.0)
    earlier = jnp.where(lane < iota((TOK, 128), 0), 1.0, 0.0).astype(BF)
    code = jnp.where(named > 0.5, dot(earlier, named.astype(BF)) + 1.0, 0.0)
    code_s[...] = code.T
    wt_s[...] = wmat.T

    m48 = iota((MSG, TOK), 0)
    part48, rank48 = part_and_rank(m48)
    want48 = (rank48 + 1).astype(F32)

    def build_e(n, carry):
        hit = code_s[pl.ds(n, 1), :] == want48
        scale = jnp.sum(jnp.where(hit, wt_s[pl.ds(n, 1), :], 0.0), axis=1, keepdims=True)
        gs_s[n] = jnp.broadcast_to(scale, (MSG, TOK))
        for q in range(4):
            e_s[n, :, q * TOK : (q + 1) * TOK] = jnp.where(hit & (part48 == q), 1.0, 0.0).astype(BF)
        return carry

    lax.fori_loop(0, SRC, build_e, 0)

    tok_in.wait()
    dout_in.wait()
    for p in range(NP):
        for q in range(4):
            cols = slice(p * W + q * Q, p * W + (q + 1) * Q)
            rhs_s[q * TOK : (q + 1) * TOK, 0:Q] = tok_v[:, cols]
            rhs_s[q * TOK : (q + 1) * TOK, Q : 2 * Q] = dout_v[:, cols]

        def pack(g, carry, p=p):
            some = pl.ds(g * 4, 4)
            rows = dot(e_s[some].reshape(4 * MSG, 4 * TOK), rhs_s[...])
            cot = rows[:, Q:] * gs_s[some].reshape(4 * MSG, TOK)
            s_s[p, some, 0:MSG, :] = rows[:, :Q].astype(BF).reshape(4, MSG, Q)
            s_s[p, some, MSG : 2 * MSG, :] = cot.astype(BF).reshape(4, MSG, Q)
            return carry

        lax.fori_loop(0, SRC // 4, pack, 0)
        if p == 0:
            pl.semaphore_wait(bar, 2 * SRC + 1)

        def send(i, carry, p=p):
            f2 = spread(i, f)
            e2 = (e + 2 * ((f + f2) % 2)) % 4
            pltpu.make_async_remote_copy(
                s_s.at[p, f2], r_s.at[p, f], ssem.at[p], rsem.at[p],
                device_id=(f2, e2), device_id_type=MESH,
            ).start()
            return carry

        lax.fori_loop(1, SRC, send, 0)
        pltpu.make_async_copy(s_s.at[p, f], r_s.at[p, f], lsem.at[p]).start()

    i_p = iota((4 * MSG, 4 * MSG), 0)
    q_p = over_msg(i_p)
    s_p, r_p = part_and_rank(i_p - MSG * q_p)
    pm_s[...] = jnp.where(iota((4 * MSG, 4 * MSG), 1) == MSG * s_p + CAP * q_p + r_p, 1.0, 0.0).astype(BF)

    w_hi = wmat.astype(BF)
    w_lo = (wmat - w_hi.astype(F32)).astype(BF)
    code_b = code.astype(BF)

    def build_et(g, carry):
        j = iota((TOK, 8 * MSG), 1)
        n = over_msg(j)
        part, rank = part_and_rank(j - MSG * n)
        rep = jnp.where(iota((TOK, 8 * MSG), 0) == n + 8 * g, 1.0, 0.0).astype(BF)
        hit = dot(code_b, rep) == (rank + 1).astype(F32)
        hi = dot(w_hi, rep)
        lo = dot(w_lo, rep)
        for q in range(4):
            here = hit & (part == q)
            rows = slice(q * TOK, (q + 1) * TOK)
            et_s[g, rows, :] = jnp.where(here, 1.0, 0.0).astype(BF)
            whi_s[g, rows, :] = jnp.where(here, hi, 0.0).astype(BF)
            wlo_s[g, rows, :] = jnp.where(here, lo, 0.0).astype(BF)
        return carry

    lax.fori_loop(0, 4, build_et, 0)
    for pp in range(2):
        for q in range(4):
            cols = pl.ds(pl.multiple_of(y * (HALF // 2) + pp * W + q * Q, Q), Q)
            dq_s[q * TOK : (q + 1) * TOK, pp * Q : (pp + 1) * Q] = dout_v[:, cols]
    gu_acc[...] = jnp.zeros_like(gu_acc)
    dh_acc[...] = jnp.zeros_like(dh_acc)
    wait_bytes(gu_s, w_sem.at[0])
    wait_bytes(dn_s, w_sem.at[1])

    def first(j):
        for n in range(3):
            cols = slice(n * 256, (n + 1) * 256)
            gu_acc[:, cols] += dot(xg_s[j, 0], gu_s[j, :, cols])
        dh_acc[...] += dot_nt(xg_s[j, 1], dn_s[j])

    def arrive(p, carry):
        mine = c * NP + p
        theirs = (1 - c) * NP + p
        wait_bytes(r_s.at[p, pl.ds(0, SRC - 1)], rsem.at[p])
        pltpu.make_async_copy(s_s.at[p, f], r_s.at[p, f], lsem.at[p]).wait()

        def unpack(g, carry):
            some = pl.ds(g * 4, 4)
            rows = pl.ds(pl.multiple_of(g * MSG, MSG), MSG)
            x = r_s[p, some, 0:MSG, :].reshape(4 * MSG, Q)
            ct = r_s[p, some, MSG : 2 * MSG, :].reshape(4 * MSG, Q)
            out = dot(pm_s[...], jnp.concatenate([x, ct], axis=1)).astype(BF)
            for q in range(4):
                xg_s[mine, 0, rows, q * Q : (q + 1) * Q] = out[q * MSG : (q + 1) * MSG, :Q]
                xg_s[mine, 1, rows, q * Q : (q + 1) * Q] = out[q * MSG : (q + 1) * MSG, Q:]
            return carry

        lax.fori_loop(0, SRC // 4, unpack, 0)
        pltpu.make_async_remote_copy(
            xg_s.at[mine], xg_s.at[mine], fs_sem.at[p], fr_sem.at[p],
            device_id=(f, mate), device_id_type=MESH,
        ).start()
        first(mine)
        wait_bytes(xg_s.at[theirs], fr_sem.at[p])
        first(theirs)
        return carry

    lax.fori_loop(0, NP, arrive, 0)

    def middle(n, carry):
        rows = pl.ds(pl.multiple_of(n * 96, 96), 96)
        gate = gu_acc[rows, 0:FH]
        up = gu_acc[rows, FH : 2 * FH]
        dh = dh_acc[rows, :]
        sig = jax.nn.sigmoid(gate)
        act = gate * sig
        hid_s[rows, :] = (act * up).astype(BF)
        slope = sig * (1.0 + gate * (1.0 - sig))
        dgu_s[rows, 0:FH] = (dh * up * slope).astype(BF)
        dgu_s[rows, FH : 2 * FH] = (dh * act).astype(BF)
        return carry

    lax.fori_loop(0, ROWS // 96, middle, 0)

    def second(t, j):
        if t < 2:
            return dot(hid_s[...], dn_s[j])
        return dot_nt(dgu_s[...], gu_s[j])

    def for_mate(t):
        base = (1 - c) * NP + 2 * ((y + t % 2) % 2)

        def one(pp, carry):
            xo_s[t, pp] = second(t, base + pp).astype(BF)
            return carry

        lax.fori_loop(0, 2, one, 0)
        pltpu.make_async_remote_copy(
            xo_s.at[t], xi_s.at[t], xs_sem.at[t], xr_sem.at[t],
            device_id=(f, mate), device_id_type=MESH,
        ).start()

    def returned(t):
        dy = t % 2
        base = c * NP + 2 * ((y + dy) % 2)
        wait_bytes(xi_s.at[t], xr_sem.at[t])

        def one(pp, carry):
            v_s[pp] = (second(t, base + pp) + xi_s[t, pp].astype(F32)).astype(BF)
            return carry

        lax.fori_loop(0, 2, one, 0)

        def pack(g, carry):
            rows = pl.ds(pl.multiple_of(g * MSG, MSG), MSG)
            some = pl.ds(g * 4, 4)
            both = [
                jnp.concatenate([v_s[pp, rows, q * Q : (q + 1) * Q] for q in range(4)], axis=0)
                for pp in range(2)
            ]
            out = dot(pm_s[...], jnp.concatenate(both, axis=1)).astype(BF)
            for pp in range(2):
                sr_s[t, some, pp * MSG : (pp + 1) * MSG, :] = out[:, pp * Q : (pp + 1) * Q].reshape(4, MSG, Q)
            return carry

        lax.fori_loop(0, SRC // 4, pack, 0)
        e2 = other if dy else e

        def send(i, carry):
            f2 = spread(i, f)
            pltpu.make_async_remote_copy(
                sr_s.at[t, f2], rr_s.at[t, f], s2_sem.at[t], r2_sem.at[t],
                device_id=(f2, e2), device_id_type=MESH,
            ).start()
            return carry

        lax.fori_loop(1 - dy, SRC, send, 0)
        if dy == 0:
            pltpu.make_async_copy(sr_s.at[t, f], rr_s.at[t, f], l2_sem.at[t // 2]).start()

    for_mate(0)
    for_mate(1)
    returned(0)
    for_mate(2)
    returned(1)
    for_mate(3)
    returned(2)
    returned(3)

    for t in range(4):
        wait_bytes(xo_s.at[t], xs_sem.at[t])

    def grads(j, carry):
        cols = pl.ds(pl.multiple_of(j * W, W), W)
        for n in range(3):
            some = slice(n * 256, (n + 1) * 256)
            gu_s[j, :, some] = dot_tn(xg_s[j, 0], dgu_s[:, some]).astype(BF)
        pltpu.make_async_copy(gu_s.at[j, :, pl.ds(0, FH)], dgate_hbm.at[0, cols, :], g_sem.at[0]).start()
        pltpu.make_async_copy(gu_s.at[j, :, pl.ds(FH, FH)], dup_hbm.at[0, cols, :], g_sem.at[0]).start()
        dn_s[j] = dot_tn(hid_s[...], xg_s[j, 1]).astype(BF)
        pltpu.make_async_copy(dn_s.at[j], ddown_hbm.at[0, :, cols], g_sem.at[1]).start()
        return carry

    lax.fori_loop(0, 2 * NP, grads, 0)

    def rhs_of(t, g):
        some = pl.ds(g * 8, 8)
        return jnp.concatenate(
            [rr_s[t, some, pp * MSG : (pp + 1) * MSG, :].reshape(8 * MSG, Q) for pp in range(2)], axis=1
        )

    mine = 2 * c + y
    flip = 2 * c + 1 - y
    theirs = 2 * (1 - c) + y
    last = 2 * (1 - c) + 1 - y

    def landed(a):
        wait_bytes(rr_s.at[2 * a, pl.ds(0, SRC - 1)], r2_sem.at[2 * a])
        pltpu.make_async_copy(sr_s.at[2 * a, f], rr_s.at[2 * a, f], l2_sem.at[a]).wait()
        wait_bytes(rr_s.at[2 * a + 1], r2_sem.at[2 * a + 1])

    def share(a):
        for pp in range(2):
            for q in range(4):
                cols = slice(pp * W + q * Q, pp * W + (q + 1) * Q)
                mq_s[a, mine, :, cols] = acc_s[q * TOK : (q + 1) * TOK, pp * Q : (pp + 1) * Q].astype(BF)
        pltpu.make_async_remote_copy(
            mq_s.at[a, mine], mq_s.at[a, mine], ys_sem.at[a], yr_sem.at[a],
            device_id=(f, other), device_id_type=MESH,
        ).start()
        pltpu.make_async_remote_copy(
            mq_s.at[a, mine], mq_s.at[a, mine], ms_sem.at[a], mr_sem.at[a],
            device_id=(f, mate), device_id_type=MESH,
        ).start()

    def forward(a):
        wait_bytes(mq_s.at[a, flip], yr_sem.at[a])
        pltpu.make_async_remote_copy(
            mq_s.at[a, flip], mq_s.at[a, flip], hs_sem.at[a], hr_sem.at[a],
            device_id=(f, mate), device_id_type=MESH,
        ).start()

    def store(a, out_hbm):
        wait_bytes(mq_s.at[a, theirs], mr_sem.at[a])
        wait_bytes(mq_s.at[a, last], hr_sem.at[a])
        for n in range(4):
            pltpu.make_async_copy(mq_s.at[a, n], out_hbm.at[:, pl.ds(n * 1024, 1024)], o_sem.at[a]).start()

    landed(0)
    acc_s[...] = jnp.zeros_like(acc_s)
    dr_s[mine] = jnp.zeros((TOK, 128), F32)

    def combine_out(g, carry):
        a, b = rhs_of(0, g), rhs_of(1, g)
        acc_s[...] += dot(whi_s[g], a) + dot(whi_s[g], b) + dot(wlo_s[g], a) + dot(wlo_s[g], b)
        prod = dot_nt(dq_s[...], a) + dot_nt(dq_s[...], b)
        kept = jnp.where(et_s[g] > 0, prod, 0.0)
        total = kept[0:TOK] + kept[TOK : 2 * TOK] + kept[2 * TOK : 3 * TOK] + kept[3 * TOK :]
        hi = total.astype(BF)
        lo = (total - hi.astype(F32)).astype(BF)
        rep = jnp.where(
            iota((8 * MSG, 128), 1) == over_msg(iota((8 * MSG, 128), 0)) + 8 * g, 1.0, 0.0
        ).astype(BF)
        dr_s[mine] += dot(hi, rep) + dot(lo, rep)
        return carry

    lax.fori_loop(0, 4, combine_out, 0)
    share(0)
    for n, e2 in enumerate((mate, other, diag)):
        pltpu.make_async_remote_copy(
            dr_s.at[mine], dr_s.at[mine], ds_sem.at[n], dr_sem.at[n],
            device_id=(f, e2), device_id_type=MESH,
        ).start()
    forward(0)
    store(0, moe_hbm)
    for n, slot in enumerate((theirs, flip, last)):
        wait_bytes(dr_s.at[slot], dr_sem.at[n])
    total = dr_s[0] + dr_s[1] + dr_s[2] + dr_s[3]
    for k in range(ids.shape[1]):
        hit = ids[:, k : k + 1] == lane
        droute_ref[:, k : k + 1] = jnp.sum(jnp.where(hit, total, 0.0), axis=1, keepdims=True)

    landed(1)
    acc_s[...] = jnp.zeros_like(acc_s)

    def combine_dx(g, carry):
        acc_s[...] += dot(et_s[g], rhs_of(2, g)) + dot(et_s[g], rhs_of(3, g))
        return carry

    lax.fori_loop(0, 4, combine_dx, 0)
    share(1)
    forward(1)
    store(1, dtok_hbm)

    for p in range(NP):
        wait_bytes(s_s.at[p, pl.ds(0, SRC - 1)], ssem.at[p])
        wait_bytes(xg_s.at[0], fs_sem.at[p])
    for t in range(4):
        wait_bytes(sr_s.at[t, pl.ds(0, SRC - 1 + t % 2)], s2_sem.at[t])
    for n in range(3):
        wait_bytes(dr_s.at[0], ds_sem.at[n])
    for a in range(2):
        for sem in (ms_sem, ys_sem, hs_sem):
            wait_bytes(mq_s.at[a, 0], sem.at[a])
        wait_bytes(mq_s.at[a], o_sem.at[a])
    wait_bytes(gu_s, g_sem.at[0])
    wait_bytes(dn_s, g_sem.at[1])


def per_device(tokens, expert_ids, route_weights, d_out, gate_weight, up_weight, down_weight):
    hbm = pl.BlockSpec(memory_space=pl.ANY)
    vmem = pl.BlockSpec(memory_space=pltpu.VMEM)
    shape = jax.ShapeDtypeStruct
    dma = pltpu.SemaphoreType.DMA
    v = pltpu.VMEM
    return pl.pallas_call(
        kernel,
        out_shape=(
            shape((TOK, D), BF), shape((TOK, D), BF), shape(route_weights.shape, F32),
            shape(gate_weight.shape, BF), shape(up_weight.shape, BF), shape(down_weight.shape, BF),
        ),
        in_specs=[vmem, vmem, hbm, hbm, hbm, hbm, hbm],
        out_specs=(hbm, hbm, vmem, hbm, hbm, hbm),
        scratch_shapes=[
            v((TOK, HALF), BF), v((TOK, HALF), BF),
            v((128, TOK), F32), v((128, TOK), F32),
            v((SRC, MSG, 4 * TOK), BF), v((SRC, MSG, TOK), F32),
            v((4, 4 * TOK, 8 * MSG), BF), v((4, 4 * TOK, 8 * MSG), BF), v((4, 4 * TOK, 8 * MSG), BF),
            v((4 * TOK, 2 * Q), BF), v((4 * MSG, 4 * MSG), BF),
            v((NP, SRC, 2 * MSG, Q), BF), v((NP, SRC, 2 * MSG, Q), BF),
            v((2 * NP, 2, ROWS, W), BF),
            v((2 * NP, W, 2 * FH), BF), v((2 * NP, FH, W), BF),
            v((ROWS, 2 * FH), F32), v((ROWS, FH), F32),
            v((ROWS, FH), BF), v((ROWS, 2 * FH), BF),
            v((4, 2, ROWS, W), BF), v((4, 2, ROWS, W), BF), v((2, ROWS, W), BF),
            v((4, SRC, 2 * MSG, Q), BF), v((4, SRC, 2 * MSG, Q), BF),
            v((4 * TOK, 2 * Q), F32), v((4 * TOK, 2 * Q), BF),
            v((2, 4, TOK, D // 4), BF), v((4, TOK, 128), F32),
            dma((2,)), dma((2,)), dma((NP,)), dma((NP,)), dma((NP,)), dma((NP,)), dma((NP,)),
            dma((4,)), dma((4,)), dma((4,)), dma((4,)), dma((2,)), dma((2,)),
            dma((2,)), dma((2,)), dma((2,)), dma((2,)), dma((2,)), dma((2,)),
            dma((3,)), dma((3,)), dma((2,)),
        ],
        compiler_params=pltpu.CompilerParams(
            collective_id=0, has_side_effects=True, vmem_limit_bytes=60 * 1024 * 1024
        ),
        cost_estimate=pl.CostEstimate(flops=11_000_000_000, bytes_accessed=23_000_000, transcendentals=200_000),
    )(expert_ids, route_weights, tokens, d_out, gate_weight, up_weight, down_weight)


def solution(mesh):
    in_specs = (
        P("fsdp", None),
        P("fsdp", None),
        P("fsdp", None),
        P("fsdp", None),
        P("fsdp", None, "expert"),
        P("fsdp", None, "expert"),
        P("fsdp", "expert", None),
    )
    out_specs = (
        P("fsdp", None),
        P("fsdp", None),
        P("fsdp", None),
        P("fsdp", None, "expert"),
        P("fsdp", None, "expert"),
        P("fsdp", "expert", None),
    )
    return jax.shard_map(
        per_device, mesh=mesh, in_specs=in_specs, out_specs=out_specs, check_vma=False
    )
```

```python
import jax
import jax.numpy as jnp
from jax import lax
from jax.experimental import pallas as pl
from jax.experimental.pallas import tpu as pltpu
from jax.sharding import PartitionSpec as P

MESH = pl.DeviceIdType.MESH
BF = jnp.bfloat16
F32 = jnp.float32

D = 4096
FH = 384
SRC = 32
TOK = 128
CAP = 12
ROWS = SRC * CAP
W = 512
MSG = 4 * CAP
Q = W // 4
HALF = D // 2
NP = HALF // W


def dot(a, b):
    return lax.dot_general(a, b, (((1,), (0,)), ((), ())), preferred_element_type=F32)


def dot_nt(a, b):
    return lax.dot_general(a, b, (((1,), (1,)), ((), ())), preferred_element_type=F32)


def dot_tn(a, b):
    return lax.dot_general(a, b, (((0,), (0,)), ((), ())), preferred_element_type=F32)


def iota(shape, dim):
    return lax.broadcasted_iota(jnp.int32, shape, dim)


def part_and_rank(m):
    part = (
        (m >= CAP).astype(jnp.int32)
        + (m >= 2 * CAP).astype(jnp.int32)
        + (m >= 3 * CAP).astype(jnp.int32)
    )
    return part, m - CAP * part


def over_msg(j):
    return (j * 1366) >> 16


def step_from(f, dz, dx, dy):
    z, x, y = lax.div(f, 8), lax.rem(lax.div(f, 2), 4), lax.rem(f, 2)
    return lax.rem(z + dz, 4) * 8 + lax.rem(x + dx, 4) * 2 + lax.rem(y + dy, 2)


def spread(i, f):
    a, b, c = lax.rem(i, 4), lax.rem(lax.div(i, 4), 4), lax.div(i, 16)
    return step_from(f, a, lax.rem(a + b, 4), lax.rem(a + b + c, 2))


def wait_bytes(ref, sem):
    pltpu.make_async_copy(ref, ref, sem).wait()


def kernel(
    ids_ref, w_ref, tok_hbm, dout_hbm, gate_hbm, up_hbm, down_hbm,
    mq_s, droute_ref, gu_s, dn_s,
    tok_v, dout_v, code_s, wt_s, e_s, gs_s, et_s, whi_s, wlo_s, rhs_s, pm_s,
    s_s, r_s, xg_s, gu_acc, dh_acc, hid_s, dgu_s,
    xo_s, xi_s, yo_s, yi_s, v_s, sr_s, rr_s, acc_s, accq_s, dq_s, dqq_s, po_s, pi_s, dr_s,
    round_sem, tok_sem, w_sem, ssem, rsem, lsem, fs_sem, fr_sem, qs_sem, qr_sem,
    xs_sem, xr_sem, ys_sem, yr_sem, s2_sem, r2_sem, l2_sem,
    ps_sem, pr_sem, ms_sem, mr_sem, ds_sem, dr_sem,
):
    f = lax.axis_index("fsdp")
    e = lax.axis_index("expert")
    y, c = lax.div(e, 2), lax.rem(e, 2)
    mate = e + 1 - 2 * c
    other = lax.rem(e + 2, 4)

    bar = pltpu.get_barrier_semaphore()
    x_line = [(step_from(f, 0, n, 0), e) for n in (1, 3, 2)]
    z_line = [(step_from(f, n, 0, 0), e) for n in (1, 3, 2)]
    y_line = [(f, other), (step_from(f, 0, 0, 1), other), (step_from(f, 0, 0, 1), e)]

    def signal(sem, devices):
        for d in devices:
            pl.semaphore_signal(sem, inc=1, device_id=d, device_id_type=MESH)

    signal(bar, z_line + x_line + y_line + [(f, mate)])

    half = pl.ds(pl.multiple_of(c * HALF, HALF), HALF)
    tok_in = pltpu.make_async_copy(tok_hbm.at[:, half], tok_v, tok_sem.at[0])
    dout_in = pltpu.make_async_copy(dout_hbm.at[:, half], dout_v, tok_sem.at[1])
    tok_in.start()
    dout_in.start()
    for j in range(2 * NP):
        cols = pl.ds(j * W, W)
        pltpu.make_async_copy(gate_hbm.at[0, cols, :], gu_s.at[j, :, pl.ds(0, FH)], w_sem.at[0]).start()
        pltpu.make_async_copy(up_hbm.at[0, cols, :], gu_s.at[j, :, pl.ds(FH, FH)], w_sem.at[0]).start()
        pltpu.make_async_copy(down_hbm.at[0, :, cols], dn_s.at[j], w_sem.at[1]).start()

    ids = ids_ref[...]
    wts = w_ref[...]
    top = ids.shape[0]
    expert = iota((128, TOK), 0)
    named = jnp.zeros((128, TOK), F32)
    wmat_t = jnp.zeros((128, TOK), F32)
    for k in range(top):
        hit = ids[k : k + 1, :] == expert
        named = named + jnp.where(hit, 1.0, 0.0)
        wmat_t = wmat_t + jnp.where(hit, wts[k : k + 1, :], 0.0)
    earlier = jnp.where(expert < iota((128, TOK), 1), 1.0, 0.0).astype(BF)
    code_s[...] = jnp.where(named > 0.5, dot(named.astype(BF), earlier) + 1.0, 0.0)
    wt_s[...] = wmat_t

    part48, rank48 = part_and_rank(iota((MSG, TOK), 0))
    want48 = (rank48 + 1).astype(F32)

    def build_e(n, carry):
        hit = code_s[pl.ds(n, 1), :] == want48
        scale = jnp.sum(jnp.where(hit, wt_s[pl.ds(n, 1), :], 0.0), axis=1, keepdims=True)
        gs_s[n] = jnp.broadcast_to(scale, (MSG, TOK))
        for q in range(4):
            e_s[n, :, q * TOK : (q + 1) * TOK] = jnp.where(hit & (part48 == q), 1.0, 0.0).astype(BF)
        return carry

    lax.fori_loop(0, SRC, build_e, 0)

    def pack(k):
        piece = 2 + y if k == 0 else k - 1
        for q in range(4):
            cols = pl.ds(pl.multiple_of(piece * W + q * Q, Q), Q)
            rhs_s[q * TOK : (q + 1) * TOK, 0:Q] = tok_v[:, cols]
            rhs_s[q * TOK : (q + 1) * TOK, Q : 2 * Q] = dout_v[:, cols]

        def some_rows(g, carry):
            some = pl.ds(g * 4, 4)
            rows = dot(e_s[some].reshape(4 * MSG, 4 * TOK), rhs_s[...])
            cot = rows[:, Q:] * gs_s[some].reshape(4 * MSG, TOK)
            s_s[k, some, 0:MSG, :] = rows[:, :Q].astype(BF).reshape(4, MSG, Q)
            s_s[k, some, MSG : 2 * MSG, :] = cot.astype(BF).reshape(4, MSG, Q)
            return carry

        lax.fori_loop(0, SRC // 4, some_rows, 0)

    def crossed(f2):
        return lax.rem(e + 2 * lax.rem(f + f2, 2), 4)

    def send(k, f2):
        pltpu.make_async_remote_copy(
            s_s.at[k, f2], r_s.at[k, f], ssem.at[k], rsem.at[k],
            device_id=(f2, e if k == 0 else crossed(f2)), device_id_type=MESH,
        ).start()

    def send_line(k):
        def one(n, carry):
            send(k, step_from(f, n, 0, 0))
            send(k, step_from(f, 0, n, 0))
            return carry

        lax.fori_loop(1, 4, one, 0)
        send(k, step_from(f, 0, 0, 1))

    def send_plane(k):
        def one(n, carry):
            a, b = lax.div(n, 3), lax.rem(n, 3)
            send(k, step_from(f, 1 + a, 1 + lax.rem(a + b, 3), 0))
            return carry

        lax.fori_loop(0, 9, one, 0)

    def send_rest(k):
        def one(n, carry):
            a, b = lax.rem(n, 4), lax.div(n, 4)
            send(k, step_from(f, a, lax.rem(a + b, 4), 1))
            return carry

        lax.fori_loop(1, 16, one, 0)

    def keep(k):
        pltpu.make_async_copy(s_s.at[k, f], r_s.at[k, f], lsem.at[k]).start()

    tok_in.wait()
    dout_in.wait()
    pack(0)
    pl.semaphore_wait(bar, 10)
    signal(round_sem.at[0], x_line)
    send_line(0)
    pack(1)
    pl.semaphore_wait(round_sem.at[0], 3)
    signal(round_sem.at[1], y_line)
    send_plane(0)
    send_line(1)
    keep(0)
    keep(1)
    pl.semaphore_wait(round_sem.at[1], 3)
    send_rest(0)
    send_plane(1)
    send_rest(1)
    pack(2)

    def send_any(i, carry):
        send(2, spread(i, f))
        return carry

    lax.fori_loop(1, SRC, send_any, 0)
    keep(2)

    i_p = iota((4 * MSG, 4 * MSG), 0)
    q_p = over_msg(i_p)
    s_p, r_p = part_and_rank(i_p - MSG * q_p)
    pm_s[...] = jnp.where(iota((4 * MSG, 4 * MSG), 1) == MSG * s_p + CAP * q_p + r_p, 1.0, 0.0).astype(BF)
    gu_acc[...] = jnp.zeros_like(gu_acc)
    dh_acc[...] = jnp.zeros_like(dh_acc)

    wmat = wt_s[...].T
    w_hi = wmat.astype(BF)
    w_lo = (wmat - w_hi.astype(F32)).astype(BF)
    code_b = code_s[...].T.astype(BF)

    def build_et(g, carry):
        j = iota((TOK, 8 * MSG), 1)
        n = over_msg(j)
        part, rank = part_and_rank(j - MSG * n)
        rep = jnp.where(iota((TOK, 8 * MSG), 0) == n + 8 * g, 1.0, 0.0).astype(BF)
        hit = dot(code_b, rep) == (rank + 1).astype(F32)
        hi = dot(w_hi, rep)
        lo = dot(w_lo, rep)
        for q in range(4):
            here = hit & (part == q)
            rows = slice(q * TOK, (q + 1) * TOK)
            et_s[g, rows, :] = jnp.where(here, 1.0, 0.0).astype(BF)
            whi_s[g, rows, :] = jnp.where(here, hi, 0.0).astype(BF)
            wlo_s[g, rows, :] = jnp.where(here, lo, 0.0).astype(BF)
        return carry

    lax.fori_loop(0, 4, build_et, 0)
    for q in range(4):
        rows = slice(q * TOK, (q + 1) * TOK)
        for pp in range(2):
            dq_s[rows, pp * Q : (pp + 1) * Q] = dout_v[:, pp * W + q * Q : pp * W + (q + 1) * Q]
        dqq_s[rows, :] = dout_v[:, pl.ds(pl.multiple_of((2 + y) * W + q * Q, Q), Q)]
    wait_bytes(gu_s, w_sem.at[0])
    wait_bytes(dn_s, w_sem.at[1])

    def first(j):
        for n in range(3):
            cols = slice(n * 256, (n + 1) * 256)
            gu_acc[:, cols] += dot(xg_s[j, 0], gu_s[j, :, cols])
        dh_acc[...] += dot_nt(xg_s[j, 1], dn_s[j])

    order = (2 + y, 0, 1, 3 - y)

    def unpack(k):
        j = c * NP + order[k]
        wait_bytes(r_s.at[k, pl.ds(0, SRC - 1)], rsem.at[k])
        pltpu.make_async_copy(s_s.at[k, f], r_s.at[k, f], lsem.at[k]).wait()

        def some_rows(g, carry):
            some = pl.ds(g * 4, 4)
            rows = pl.ds(pl.multiple_of(g * MSG, MSG), MSG)
            x = r_s[k, some, 0:MSG, :].reshape(4 * MSG, Q)
            ct = r_s[k, some, MSG : 2 * MSG, :].reshape(4 * MSG, Q)
            out = dot(pm_s[...], jnp.concatenate([x, ct], axis=1)).astype(BF)
            for q in range(4):
                xg_s[j, 0, rows, q * Q : (q + 1) * Q] = out[q * MSG : (q + 1) * MSG, :Q]
                xg_s[j, 1, rows, q * Q : (q + 1) * Q] = out[q * MSG : (q + 1) * MSG, Q:]
            return carry

        lax.fori_loop(0, SRC // 4, some_rows, 0)

    def to_mate(k):
        j = c * NP + order[k]
        pltpu.make_async_remote_copy(
            xg_s.at[j], xg_s.at[j], fs_sem.at[k], fr_sem.at[k],
            device_id=(f, mate), device_id_type=MESH,
        ).start()

    def from_mate(k):
        j = (1 - c) * NP + order[k]
        wait_bytes(xg_s.at[j], fr_sem.at[k])
        first(j)

    unpack(0)
    here = c * NP + order[0]
    pltpu.make_async_remote_copy(
        xg_s.at[here], xg_s.at[here], qs_sem, qr_sem, device_id=(f, other), device_id_type=MESH
    ).start()
    to_mate(0)
    first(here)
    from_mate(0)
    unpack(1)
    to_mate(1)
    first(c * NP)
    from_mate(1)
    unpack(2)
    to_mate(2)
    first(c * NP + 1)
    from_mate(2)
    there = c * NP + order[3]
    wait_bytes(xg_s.at[there], qr_sem)
    to_mate(3)
    first(there)
    from_mate(3)

    def middle(n, carry):
        rows = pl.ds(pl.multiple_of(n * 96, 96), 96)
        gate = gu_acc[rows, 0:FH]
        up = gu_acc[rows, FH : 2 * FH]
        dh = dh_acc[rows, :]
        sig = jax.nn.sigmoid(gate)
        act = gate * sig
        hid_s[rows, :] = (act * up).astype(BF)
        slope = sig * (1.0 + gate * (1.0 - sig))
        dgu_s[rows, 0:FH] = (dh * up * slope).astype(BF)
        dgu_s[rows, FH : 2 * FH] = (dh * act).astype(BF)
        return carry

    lax.fori_loop(0, ROWS // 96, middle, 0)

    back = (3 - y, 0, 1, 2 + y)

    def second(a, j):
        if a == 0:
            return dot(hid_s[...], dn_s[j])
        return dot_nt(dgu_s[...], gu_s[j])

    def for_mate(a, k):
        t = 4 * a + k
        xo_s[t] = second(a, (1 - c) * NP + back[k]).astype(BF)
        pltpu.make_async_remote_copy(
            xo_s.at[t], xi_s.at[t], xs_sem.at[t], xr_sem.at[t],
            device_id=(f, mate), device_id_type=MESH,
        ).start()

    def chip_sum(a, k):
        t = 4 * a + k
        own = second(a, c * NP + back[k])
        wait_bytes(xi_s.at[t], xr_sem.at[t])
        return own + xi_s[t].astype(F32)

    def for_other(a):
        yo_s[a] = chip_sum(a, 0).astype(BF)
        pltpu.make_async_remote_copy(
            yo_s.at[a], yi_s.at[a], ys_sem.at[a], yr_sem.at[a],
            device_id=(f, other), device_id_type=MESH,
        ).start()

    def returned(a, k):
        t = 3 * a + k - 1
        total = chip_sum(a, k)
        if k == 3:
            wait_bytes(yi_s.at[a], yr_sem.at[a])
            total = total + yi_s[a].astype(F32)
        v_s[...] = total.astype(BF)

        def some_rows(g, carry):
            rows = pl.ds(pl.multiple_of(g * MSG, MSG), MSG)
            some = pl.ds(g * 4, 4)
            both = jnp.concatenate([v_s[rows, q * Q : (q + 1) * Q] for q in range(4)], axis=0)
            sr_s[t, some] = dot(pm_s[...], both).astype(BF).reshape(4, MSG, Q)
            return carry

        lax.fori_loop(0, SRC // 4, some_rows, 0)

        def send_back(i, carry):
            f2 = spread(i, f)
            pltpu.make_async_remote_copy(
                sr_s.at[t, f2], rr_s.at[t, f], s2_sem.at[t], r2_sem.at[t],
                device_id=(f2, e if k == 3 else crossed(f2)), device_id_type=MESH,
            ).start()
            return carry

        lax.fori_loop(1, SRC, send_back, 0)
        pltpu.make_async_copy(sr_s.at[t, f], rr_s.at[t, f], l2_sem.at[t]).start()

    for_mate(0, 0)
    for_mate(0, 1)
    for_other(0)
    for_mate(0, 2)
    returned(0, 1)
    for_mate(0, 3)
    returned(0, 2)
    for_mate(1, 0)
    for_mate(1, 1)
    for_other(1)
    returned(0, 3)
    for_mate(1, 2)
    returned(1, 1)
    for_mate(1, 3)
    returned(1, 2)
    returned(1, 3)

    def grads(j, carry):
        for n in range(3):
            some = slice(n * 256, (n + 1) * 256)
            gu_s[j, :, some] = dot_tn(xg_s[j, 0], dgu_s[:, some]).astype(BF)
        dn_s[j] = dot_tn(hid_s[...], xg_s[j, 1]).astype(BF)
        return carry

    lax.fori_loop(0, 2 * NP, grads, 0)

    def landed(a, k):
        t = 3 * a + k
        wait_bytes(rr_s.at[t, pl.ds(0, SRC - 1)], r2_sem.at[t])
        pltpu.make_async_copy(sr_s.at[t, f], rr_s.at[t, f], l2_sem.at[t]).wait()

    def block(t, g):
        return rr_s[t, pl.ds(g * 8, 8)].reshape(8 * MSG, Q)

    def pair(a, g):
        return jnp.concatenate([block(3 * a, g), block(3 * a + 1, g)], axis=1)

    base = c * NP

    def share_partial(a):
        for pp in range(2):
            for q in range(4):
                po_s[a, pp, :, q * Q : (q + 1) * Q] = acc_s[
                    q * TOK : (q + 1) * TOK, pp * Q : (pp + 1) * Q
                ].astype(BF)
        pltpu.make_async_remote_copy(
            po_s.at[a], pi_s.at[a], ps_sem.at[2 * a], pr_sem.at[2 * a],
            device_id=(f, other), device_id_type=MESH,
        ).start()

    def share_whole(a):
        n = base + 2 + y
        for q in range(4):
            mq_s[a, n, :, q * Q : (q + 1) * Q] = accq_s[q * TOK : (q + 1) * TOK, :].astype(BF)
        pltpu.make_async_remote_copy(
            mq_s.at[a, n], mq_s.at[a, n], ps_sem.at[2 * a + 1], pr_sem.at[2 * a + 1],
            device_id=(f, other), device_id_type=MESH,
        ).start()

    def hand_over(a, h):
        some = pl.ds(base + 2 * h, 2)
        pltpu.make_async_remote_copy(
            mq_s.at[a, some], mq_s.at[a, some], ms_sem.at[2 * a + h], mr_sem.at[2 * a + h],
            device_id=(f, mate), device_id_type=MESH,
        ).start()

    def add_partial(a):
        wait_bytes(pi_s.at[a], pr_sem.at[2 * a])
        mq_s[a, pl.ds(base, 2)] = (po_s[a].astype(F32) + pi_s[a].astype(F32)).astype(BF)
        hand_over(a, 0)

    def pass_whole(a):
        wait_bytes(mq_s.at[a, base + 3 - y], pr_sem.at[2 * a + 1])
        hand_over(a, 1)

    def complete(a):
        for h in range(2):
            wait_bytes(mq_s.at[a, pl.ds((1 - c) * NP + 2 * h, 2)], mr_sem.at[2 * a + h])

    for k in range(3):
        landed(0, k)
    acc_s[...] = jnp.zeros_like(acc_s)
    accq_s[...] = jnp.zeros_like(accq_s)
    dr_s[0] = jnp.zeros((TOK, 128), F32)

    def combine_out(g, carry):
        u, v = pair(0, g), block(2, g)
        acc_s[...] += dot(whi_s[g], u) + dot(wlo_s[g], u)
        accq_s[...] += dot(whi_s[g], v) + dot(wlo_s[g], v)
        prod = dot_nt(dq_s[...], u) + dot_nt(dqq_s[...], v)
        kept = jnp.where(et_s[g] > 0, prod, 0.0)
        total = kept[0:TOK] + kept[TOK : 2 * TOK] + kept[2 * TOK : 3 * TOK] + kept[3 * TOK :]
        hi = total.astype(BF)
        lo = (total - hi.astype(F32)).astype(BF)
        rep = jnp.where(
            iota((8 * MSG, 128), 1) == over_msg(iota((8 * MSG, 128), 0)) + 8 * g, 1.0, 0.0
        ).astype(BF)
        dr_s[0] += dot(hi, rep) + dot(lo, rep)
        return carry

    lax.fori_loop(0, 4, combine_out, 0)
    share_partial(0)
    share_whole(0)

    def sum_route(n, device):
        copy = pltpu.make_async_remote_copy(
            dr_s.at[2 * n], dr_s.at[2 * n + 1], ds_sem.at[n], dr_sem.at[n],
            device_id=(f, device), device_id_type=MESH,
        )
        copy.start()
        return copy

    route = sum_route(0, other)
    add_partial(0)
    pass_whole(0)
    route.wait()
    dr_s[2] = dr_s[0] + dr_s[1]
    route = sum_route(1, mate)
    route.wait()
    total = (dr_s[2] + dr_s[3]).T
    for k in range(top):
        hit = ids_ref[k : k + 1, :] == expert
        droute_ref[k : k + 1, :] = jnp.sum(jnp.where(hit, total, 0.0), axis=0, keepdims=True)

    landed(1, 0)
    landed(1, 1)
    acc_s[...] = jnp.zeros_like(acc_s)
    accq_s[...] = jnp.zeros_like(accq_s)

    def combine_pair(g, carry):
        acc_s[...] += dot(et_s[g], pair(1, g))
        return carry

    lax.fori_loop(0, 4, combine_pair, 0)
    share_partial(1)
    landed(1, 2)

    def combine_whole(g, carry):
        accq_s[...] += dot(et_s[g], block(5, g))
        return carry

    lax.fori_loop(0, 4, combine_whole, 0)
    share_whole(1)
    add_partial(1)
    pass_whole(1)
    complete(0)
    complete(1)

    for k in range(3):
        wait_bytes(s_s.at[k, pl.ds(0, SRC - 1)], ssem.at[k])
    wait_bytes(xg_s.at[0], qs_sem)
    for k in range(4):
        wait_bytes(xg_s.at[0], fs_sem.at[k])
    for t in range(8):
        wait_bytes(xo_s.at[t], xs_sem.at[t])
    for t in range(6):
        wait_bytes(sr_s.at[t, pl.ds(0, SRC - 1)], s2_sem.at[t])
    for a in range(2):
        wait_bytes(yo_s.at[a], ys_sem.at[a])
        wait_bytes(po_s.at[a], ps_sem.at[2 * a])
        wait_bytes(mq_s.at[a, 0], ps_sem.at[2 * a + 1])
        for h in range(2):
            wait_bytes(mq_s.at[a, pl.ds(0, 2)], ms_sem.at[2 * a + h])


def store_kernel(
    mq_ref, droute_ref, gu_ref, dn_ref,
    moe_hbm, dtok_hbm, out_ref, dgate_hbm, dup_hbm, ddown_hbm, sem,
):
    copies = []
    for j in range(2 * NP):
        cols = pl.ds(j * W, W)
        copies += [
            (gu_ref.at[j, :, pl.ds(0, FH)], dgate_hbm.at[0, cols, :]),
            (gu_ref.at[j, :, pl.ds(FH, FH)], dup_hbm.at[0, cols, :]),
            (dn_ref.at[j], ddown_hbm.at[0, :, cols]),
        ]
    for a, out_hbm in enumerate((moe_hbm, dtok_hbm)):
        for n in range(2 * NP):
            copies.append((mq_ref.at[a, n], out_hbm.at[:, pl.ds(n * W, W)]))
    copies = [pltpu.make_async_copy(s, d, sem.at[n]) for n, (s, d) in enumerate(copies)]
    for one in copies:
        one.start()
    out_ref[...] = droute_ref[...]
    for one in copies:
        one.wait()


def per_device(tokens, expert_ids, route_weights, d_out, gate_weight, up_weight, down_weight):
    hbm = pl.BlockSpec(memory_space=pl.ANY)
    vmem = pl.BlockSpec(memory_space=pltpu.VMEM)
    shape = jax.ShapeDtypeStruct
    dma = pltpu.SemaphoreType.DMA
    v = pltpu.VMEM
    top = route_weights.shape[1]
    mq, droute, gu, dn = pl.pallas_call(
        kernel,
        out_shape=(
            v((2, 2 * NP, TOK, W), BF), v((top, TOK), F32),
            v((2 * NP, W, 2 * FH), BF), v((2 * NP, FH, W), BF),
        ),
        in_specs=[vmem, vmem, hbm, hbm, hbm, hbm, hbm],
        out_specs=(vmem, vmem, vmem, vmem),
        scratch_shapes=[
            v((TOK, HALF), BF), v((TOK, HALF), BF),
            v((128, TOK), F32), v((128, TOK), F32),
            v((SRC, MSG, 4 * TOK), BF), v((SRC, MSG, TOK), F32),
            v((4, 4 * TOK, 8 * MSG), BF), v((4, 4 * TOK, 8 * MSG), BF), v((4, 4 * TOK, 8 * MSG), BF),
            v((4 * TOK, 2 * Q), BF), v((4 * MSG, 4 * MSG), BF),
            v((3, SRC, 2 * MSG, Q), BF), v((3, SRC, 2 * MSG, Q), BF),
            v((2 * NP, 2, ROWS, W), BF),
            v((ROWS, 2 * FH), F32), v((ROWS, FH), F32),
            v((ROWS, FH), BF), v((ROWS, 2 * FH), BF),
            v((8, ROWS, W), BF), v((8, ROWS, W), BF),
            v((2, ROWS, W), BF), v((2, ROWS, W), BF), v((ROWS, W), BF),
            v((6, SRC, MSG, Q), BF), v((6, SRC, MSG, Q), BF),
            v((4 * TOK, 2 * Q), F32), v((4 * TOK, Q), F32),
            v((4 * TOK, 2 * Q), BF), v((4 * TOK, Q), BF),
            v((2, 2, TOK, W), BF), v((2, 2, TOK, W), BF),
            v((4, TOK, 128), F32),
            pltpu.SemaphoreType.REGULAR((2,)),
            dma((2,)), dma((2,)), dma((3,)), dma((3,)), dma((3,)), dma((4,)), dma((4,)), dma, dma,
            dma((8,)), dma((8,)), dma((2,)), dma((2,)), dma((6,)), dma((6,)), dma((6,)),
            dma((4,)), dma((4,)), dma((4,)), dma((4,)), dma((2,)), dma((2,)),
        ],
        compiler_params=pltpu.CompilerParams(
            collective_id=0, has_side_effects=True, vmem_limit_bytes=46 * 1024 * 1024
        ),
        cost_estimate=pl.CostEstimate(flops=11_000_000_000, bytes_accessed=12_000_000, transcendentals=200_000),
    )(expert_ids.T, route_weights.T, tokens, d_out, gate_weight, up_weight, down_weight)
    moe, dtok, droute, dgate, dup, ddown = pl.pallas_call(
        store_kernel,
        out_shape=(
            shape((TOK, D), BF), shape((TOK, D), BF), shape((top, TOK), F32),
            shape(gate_weight.shape, BF), shape(up_weight.shape, BF), shape(down_weight.shape, BF),
        ),
        in_specs=[vmem, vmem, vmem, vmem],
        out_specs=(hbm, hbm, vmem, hbm, hbm, hbm),
        scratch_shapes=[dma((10 * NP,))],
        compiler_params=pltpu.CompilerParams(vmem_limit_bytes=1024 * 1024),
        cost_estimate=pl.CostEstimate(flops=0, bytes_accessed=12_000_000, transcendentals=0),
    )(mq, droute, gu, dn)
    return moe, dtok, droute.T, dgate, dup, ddown


def solution(mesh):
    in_specs = (
        P("fsdp", None),
        P("fsdp", None),
        P("fsdp", None),
        P("fsdp", None),
        P("fsdp", None, "expert"),
        P("fsdp", None, "expert"),
        P("fsdp", "expert", None),
    )
    out_specs = (
        P("fsdp", None),
        P("fsdp", None),
        P("fsdp", None),
        P("fsdp", None, "expert"),
        P("fsdp", None, "expert"),
        P("fsdp", "expert", None),
    )
    return jax.shard_map(
        per_device, mesh=mesh, in_specs=in_specs, out_specs=out_specs, check_vma=False
    )
```

```python
import jax
import jax.numpy as jnp
from jax import lax
from jax.experimental import pallas as pl
from jax.experimental.pallas import tpu as pltpu
from jax.sharding import PartitionSpec as P

MESH = pl.DeviceIdType.MESH
BF = jnp.bfloat16
F32 = jnp.float32

D = 4096
FH = 384
SRC = 32
TOK = 128
CAP = 12
ROWS = SRC * CAP
W = 512
MSG = 4 * CAP
Q = W // 4
HALF = D // 2
NP = HALF // W


def dot(a, b):
    return lax.dot_general(a, b, (((1,), (0,)), ((), ())), preferred_element_type=F32)


def dot_nt(a, b):
    return lax.dot_general(a, b, (((1,), (1,)), ((), ())), preferred_element_type=F32)


def dot_tn(a, b):
    return lax.dot_general(a, b, (((0,), (0,)), ((), ())), preferred_element_type=F32)


def iota(shape, dim):
    return lax.broadcasted_iota(jnp.int32, shape, dim)


def over_cap(j):
    return (j * 5462) >> 16


def to_message(rows, s):
    some = slice(s * CAP, (s + 1) * CAP)
    return jnp.concatenate([rows[some, q * Q : (q + 1) * Q] for q in range(4)], axis=0)


def from_messages(msgs, q):
    return jnp.concatenate([msgs[s, q * CAP : (q + 1) * CAP, :] for s in range(4)], axis=0)


def step_from(f, dz, dx, dy):
    z, x, y = lax.div(f, 8), lax.rem(lax.div(f, 2), 4), lax.rem(f, 2)
    return lax.rem(z + dz, 4) * 8 + lax.rem(x + dx, 4) * 2 + lax.rem(y + dy, 2)


def spread(i, f):
    a, b, c = lax.rem(i, 4), lax.rem(lax.div(i, 4), 4), lax.div(i, 16)
    return step_from(f, a, lax.rem(a + b, 4), lax.rem(a + b + c, 2))


def wait_bytes(ref, sem):
    pltpu.make_async_copy(ref, ref, sem).wait()


def kernel(
    ids_hbm, w_hbm, tok_hbm, dout_hbm, gate_hbm, up_hbm, down_hbm,
    mq_s, droute_ref, gu_s, dn_s,
    ids_s, w_s, tok_v, dout_v, e_s, gs_s, et_s, whi_s, wlo_s, t_s,
    sq_s, rq_s, sb_s, rb_s, xg_s, gu_acc, dh_acc, hid_s, dgu_s,
    xo_s, xi_s, yo_s, yi_s, v_s, vq_s, sr_s, rr_s, u_s, po_s, pi_s, dr_s,
    round_sem, tok_sem, w_sem, ssem, rsem, lsem, fs_sem, fr_sem, qs_sem, qr_sem,
    xs_sem, xr_sem, ys_sem, yr_sem, s2_sem, r2_sem, l2_sem,
    ps_sem, pr_sem, ms_sem, mr_sem, ds_sem, dr_sem,
):
    f = lax.axis_index("fsdp")
    e = lax.axis_index("expert")
    y, c = lax.div(e, 2), lax.rem(e, 2)
    mate = e + 1 - 2 * c
    other = lax.rem(e + 2, 4)

    bar = pltpu.get_barrier_semaphore()
    x_line = [(step_from(f, 0, n, 0), e) for n in (1, 3, 2)]
    z_line = [(step_from(f, n, 0, 0), e) for n in (1, 3, 2)]
    y_line = [(f, other), (step_from(f, 0, 0, 1), other), (step_from(f, 0, 0, 1), e)]

    def signal(sem, devices):
        for d in devices:
            pl.semaphore_signal(sem, inc=1, device_id=d, device_id_type=MESH)

    signal(bar, z_line + x_line + y_line + [(f, mate)])

    ids_in = pltpu.make_async_copy(ids_hbm, ids_s, tok_sem.at[2])
    w_in = pltpu.make_async_copy(w_hbm, w_s, tok_sem.at[3])
    ids_in.start()
    w_in.start()
    half = pl.ds(pl.multiple_of(c * HALF, HALF), HALF)
    tok_in = pltpu.make_async_copy(tok_hbm.at[:, half], tok_v, tok_sem.at[0])
    dout_in = pltpu.make_async_copy(dout_hbm.at[:, half], dout_v, tok_sem.at[1])
    tok_in.start()
    dout_in.start()

    ids_in.wait()
    w_in.wait()
    top = ids_s.shape[0]
    expert = iota((128, TOK), 0)
    named = jnp.zeros((128, TOK), F32)
    wmat = jnp.zeros((128, TOK), F32)
    for k in range(top):
        hit = ids_s[k : k + 1, :] == expert
        named = named + jnp.where(hit, 1.0, 0.0)
        wmat = wmat + jnp.where(hit, w_s[k : k + 1, :], 0.0)
    earlier = jnp.where(expert < iota((128, TOK), 1), 1.0, 0.0).astype(BF)
    code = jnp.where(named > 0.5, dot(named.astype(BF), earlier) + 1.0, 0.0)
    w_hi = wmat.astype(BF)
    w_mid = (wmat - w_hi.astype(F32)).astype(BF)
    w_lo = (wmat - w_hi.astype(F32) - w_mid.astype(F32)).astype(BF)

    slot = iota((ROWS, 128), 0)
    owner = over_cap(slot)
    rep = jnp.where(owner == iota((ROWS, 128), 1), 1.0, 0.0).astype(BF)
    fills = dot(rep, code.astype(BF)) == (slot - CAP * owner + 1).astype(F32)
    e_s[...] = jnp.where(fills, 1.0, 0.0).astype(BF)
    scale = (dot(rep, w_hi) + dot(rep, w_mid)) + dot(rep, w_lo)
    scale = jnp.sum(jnp.where(fills, scale, 0.0), axis=1, keepdims=True)
    gs_s[...] = jnp.broadcast_to(scale, (ROWS, 128))

    def rows_of(h, piece, at):
        for n in range(2):
            cols = pl.ds(pl.multiple_of(piece * W + n * 256, 256), 256)
            here = at * W + n * 256
            if h == 0:
                t_s[:, here : here + 256] = dot(e_s[...], tok_v[:, cols])
            else:
                cot = dot(e_s[...], dout_v[:, cols])
                for m in range(2):
                    t_s[:, here + m * Q : here + (m + 1) * Q] = cot[:, m * Q : (m + 1) * Q] * gs_s[...]

    def pack_one(h):
        for at in range(2):
            rows_of(h, 2 + lax.rem(y + f + at, 2), at)

        def some_rows(g, carry):
            rows = pl.ds(pl.multiple_of(g * MSG, MSG), MSG)
            for s in range(4):
                some = t_s[rows, (s % 2) * W : (s % 2 + 1) * W]
                sq_s[h, g * 4 + s] = to_message(some, s).astype(BF)
            return carry

        lax.fori_loop(0, SRC // 4, some_rows, 0)

    def pack_two(h):
        for at in range(2):
            rows_of(h, at, at)

        def some_rows(g, carry):
            rows = pl.ds(pl.multiple_of(g * MSG, MSG), MSG)
            for at in range(2):
                some = t_s[rows, at * W : (at + 1) * W]
                for s in range(4):
                    sb_s[h, g * 4 + s, at * MSG : (at + 1) * MSG, :] = to_message(some, s).astype(BF)
            return carry

        lax.fori_loop(0, SRC // 4, some_rows, 0)

    def crossed(f2):
        return lax.rem(e + 2 * lax.rem(f + f2, 2), 4)

    def send_one(h, f2):
        pltpu.make_async_remote_copy(
            sq_s.at[h, f2], rq_s.at[h, f], ssem.at[h], rsem.at[h],
            device_id=(f2, crossed(f2)), device_id_type=MESH,
        ).start()

    def send_two(h, f2):
        pltpu.make_async_remote_copy(
            sb_s.at[h, f2], rb_s.at[h, f], ssem.at[2 + h], rsem.at[2 + h],
            device_id=(f2, crossed(f2)), device_id_type=MESH,
        ).start()

    def to_line(send):
        def one(n, carry):
            send(0, step_from(f, n, 0, 0))
            send(0, step_from(f, 0, n, 0))
            return carry

        lax.fori_loop(1, 4, one, 0)
        send(0, step_from(f, 0, 0, 1))

    def to_plane(send):
        def one(n, carry):
            a, b = lax.div(n, 3), lax.rem(n, 3)
            send(0, step_from(f, 1 + a, 1 + lax.rem(a + b, 3), 0))
            return carry

        lax.fori_loop(0, 9, one, 0)

    def to_rest(send):
        def one(n, carry):
            a, b = lax.rem(n, 4), lax.div(n, 4)
            send(0, step_from(f, a, lax.rem(a + b, 4), 1))
            return carry

        lax.fori_loop(1, 16, one, 0)

    def to_all(send, h):
        def one(n, carry):
            send(h, spread(n, f))
            return carry

        lax.fori_loop(1, SRC, one, 0)

    tok_in.wait()
    pack_one(0)
    pl.semaphore_wait(bar, 10)
    signal(round_sem.at[0], x_line)
    to_line(send_one)
    pack_two(0)
    pl.semaphore_wait(round_sem.at[0], 3)
    signal(round_sem.at[1], y_line)
    to_plane(send_one)
    to_line(send_two)
    dout_in.wait()
    pack_one(1)
    pl.semaphore_wait(round_sem.at[1], 3)
    to_rest(send_one)
    to_plane(send_two)
    to_rest(send_two)
    to_all(send_one, 1)
    pack_two(1)
    to_all(send_two, 1)
    for h in range(2):
        pltpu.make_async_copy(sq_s.at[h, f], rq_s.at[h, f], lsem.at[h]).start()
        pltpu.make_async_copy(sb_s.at[h, f], rb_s.at[h, f], lsem.at[2 + h]).start()
    for j in range(2 * NP):
        cols = pl.ds(j * W, W)
        pltpu.make_async_copy(gate_hbm.at[0, cols, :], gu_s.at[j, :, pl.ds(0, FH)], w_sem.at[0]).start()
        pltpu.make_async_copy(up_hbm.at[0, cols, :], gu_s.at[j, :, pl.ds(FH, FH)], w_sem.at[0]).start()
        pltpu.make_async_copy(down_hbm.at[0, :, cols], dn_s.at[j], w_sem.at[1]).start()

    gu_acc[...] = jnp.zeros_like(gu_acc)
    dh_acc[...] = jnp.zeros_like(dh_acc)
    slot_t = iota((TOK, ROWS), 1)
    owner_t = over_cap(slot_t)
    rep_t = jnp.where(owner_t == iota((TOK, ROWS), 0), 1.0, 0.0).astype(BF)
    fills_t = dot(code.T.astype(BF), rep_t) == (slot_t - CAP * owner_t + 1).astype(F32)
    et_s[...] = jnp.where(fills_t, 1.0, 0.0).astype(BF)
    wmat_t = wmat.T
    w_hi_t = wmat_t.astype(BF)
    w_lo_t = (wmat_t - w_hi_t.astype(F32)).astype(BF)
    whi_s[...] = jnp.where(fills_t, dot(w_hi_t, rep_t), 0.0).astype(BF)
    wlo_s[...] = jnp.where(fills_t, dot(w_lo_t, rep_t), 0.0).astype(BF)
    wait_bytes(gu_s, w_sem.at[0])
    wait_bytes(dn_s, w_sem.at[1])

    def first(h, j):
        if h == 1:
            dh_acc[...] += dot_nt(xg_s[j, 1], dn_s[j])
            return
        for n in range(3):
            cols = slice(n * 256, (n + 1) * 256)
            gu_acc[:, cols] += dot(xg_s[j, 0], gu_s[j, :, cols])

    order = (2 + y, 0, 1, 3 - y)
    base = c * NP
    far = (1 - c) * NP

    def unpack(h, msgs, n, pieces):
        wait_bytes(msgs.at[h, pl.ds(0, SRC - 1)], rsem.at[2 * n + h])
        sent = (sq_s, sb_s)[n]
        pltpu.make_async_copy(sent.at[h, f], msgs.at[h, f], lsem.at[2 * n + h]).wait()

        def some_rows(g, carry):
            rows = pl.ds(pl.multiple_of(g * MSG, MSG), MSG)
            some = msgs[h, pl.ds(g * 4, 4)].astype(F32)
            for at, piece in enumerate(pieces):
                part = some[:, at * MSG : (at + 1) * MSG, :]
                for q in range(4):
                    xg_s[base + piece, h, rows, q * Q : (q + 1) * Q] = from_messages(part, q).astype(BF)
            return carry

        lax.fori_loop(0, SRC // 4, some_rows, 0)

    def to_mate(h, k):
        j = base + order[k]
        pltpu.make_async_remote_copy(
            xg_s.at[j, h], xg_s.at[j, h], fs_sem.at[4 * h + k], fr_sem.at[4 * h + k],
            device_id=(f, mate), device_id_type=MESH,
        ).start()

    def from_mate(h, k):
        j = far + order[k]
        wait_bytes(xg_s.at[j, h], fr_sem.at[4 * h + k])
        first(h, j)

    def get_one(h):
        j = base + order[0]
        unpack(h, rq_s, 0, order[0:1])
        pltpu.make_async_remote_copy(
            xg_s.at[j, h], xg_s.at[j, h], qs_sem.at[h], qr_sem.at[h],
            device_id=(f, other), device_id_type=MESH,
        ).start()
        to_mate(h, 0)

    def get_rest(h):
        first(h, base + order[0])
        from_mate(h, 0)
        unpack(h, rb_s, 1, order[1:3])
        to_mate(h, 1)
        to_mate(h, 2)
        first(h, base + order[1])
        first(h, base + order[2])
        there = base + order[3]
        wait_bytes(xg_s.at[there, h], qr_sem.at[h])
        to_mate(h, 3)
        first(h, there)
        for k in range(1, 4):
            from_mate(h, k)

    def middle(h):
        def some_rows(n, carry):
            rows = pl.ds(pl.multiple_of(n * 96, 96), 96)
            gate = gu_acc[rows, 0:FH]
            up = gu_acc[rows, FH : 2 * FH]
            sig = jax.nn.sigmoid(gate)
            act = gate * sig
            if h == 0:
                hid_s[rows, :] = (act * up).astype(BF)
                return carry
            dh = dh_acc[rows, :]
            slope = sig * (1.0 + gate * (1.0 - sig))
            dgu_s[rows, 0:FH] = (dh * up * slope).astype(BF)
            dgu_s[rows, FH : 2 * FH] = (dh * act).astype(BF)
            return carry

        lax.fori_loop(0, ROWS // 96, some_rows, 0)

    back = ((0, 1, 2, 3), (3 - y, 0, 1, 2 + y))

    def second(a, j):
        if a == 0:
            return dot(hid_s[...], dn_s[j])
        return dot_nt(dgu_s[...], gu_s[j])

    def for_mate(a, k):
        t = 4 * a + k
        xo_s[t] = second(a, far + back[a][k]).astype(BF)
        pltpu.make_async_remote_copy(
            xo_s.at[t], xi_s.at[t], xs_sem.at[t], xr_sem.at[t],
            device_id=(f, mate), device_id_type=MESH,
        ).start()

    def chip_sum(a, k):
        t = 4 * a + k
        own = second(a, base + back[a][k])
        wait_bytes(xi_s.at[t], xr_sem.at[t])
        return own + xi_s[t].astype(F32)

    def send_back(t):
        def some_rows(g, carry):
            some = v_s[pl.ds(pl.multiple_of(g * MSG, MSG), MSG), :]
            for s in range(4):
                sr_s[t, g * 4 + s] = to_message(some, s).astype(BF)
            return carry

        lax.fori_loop(0, SRC // 4, some_rows, 0)

        def one(i, carry):
            f2 = spread(i, f)
            pltpu.make_async_remote_copy(
                sr_s.at[t, f2], rr_s.at[t, f], s2_sem.at[t], r2_sem.at[t],
                device_id=(f2, crossed(f2)), device_id_type=MESH,
            ).start()
            return carry

        lax.fori_loop(1, SRC, one, 0)
        pltpu.make_async_copy(sr_s.at[t, f], rr_s.at[t, f], l2_sem.at[t]).start()

    def returned(a, k):
        v_s[...] = chip_sum(a, k)
        send_back(3 * a + k)

    def for_other():
        same = lax.rem(over_cap(iota((ROWS, W), 0)) + f, 2) == 0
        a, b = chip_sum(1, 0), chip_sum(1, 3)
        yo_s[...] = jnp.where(same, a, b).astype(BF)
        vq_s[...] = jnp.where(same, b, a)
        pltpu.make_async_remote_copy(
            yo_s, yi_s, ys_sem, yr_sem, device_id=(f, other), device_id_type=MESH
        ).start()

    def both_chips():
        wait_bytes(yi_s, yr_sem)
        v_s[...] = vq_s[...] + yi_s[...].astype(F32)
        send_back(6)

    def grads(j, carry):
        for n in range(3):
            some = slice(n * 256, (n + 1) * 256)
            gu_s[j, :, some] = dot_tn(xg_s[j, 0], dgu_s[:, some]).astype(BF)
        dn_s[j] = dot_tn(hid_s[...], xg_s[j, 1]).astype(BF)
        return carry

    def landed(t):
        wait_bytes(rr_s.at[t, pl.ds(0, SRC - 1)], r2_sem.at[t])
        pltpu.make_async_copy(sr_s.at[t, f], rr_s.at[t, f], l2_sem.at[t]).wait()

        def some_rows(g, carry):
            rows = pl.ds(pl.multiple_of(g * MSG, MSG), MSG)
            msgs = rr_s[t, pl.ds(g * 4, 4)].astype(F32)
            for q in range(4):
                u_s[t, rows, q * Q : (q + 1) * Q] = from_messages(msgs, q).astype(BF)
            return carry

        lax.fori_loop(0, SRC // 4, some_rows, 0)

    def combined(t):
        u = u_s[t]
        if t >= 4:
            return dot(et_s[...], u).astype(BF)
        return (dot(whi_s[...], u) + dot(wlo_s[...], u)).astype(BF)

    def share_partial(n):
        for k in range(2):
            landed(2 * n + k)
            po_s[n, k] = combined(2 * n + k)
        pltpu.make_async_remote_copy(
            po_s.at[n], pi_s.at[n], ps_sem.at[n], pr_sem.at[n],
            device_id=(f, other), device_id_type=MESH,
        ).start()

    def share_whole():
        n = base + 2 + y
        landed(6)
        mq_s[1, n] = combined(6)
        pltpu.make_async_remote_copy(
            mq_s.at[1, n], mq_s.at[1, n], ps_sem.at[3], pr_sem.at[3],
            device_id=(f, other), device_id_type=MESH,
        ).start()

    def hand_over(n):
        some = pl.ds(base + 2 * (n % 2), 2)
        pltpu.make_async_remote_copy(
            mq_s.at[n // 2, some], mq_s.at[n // 2, some], ms_sem.at[n], mr_sem.at[n],
            device_id=(f, mate), device_id_type=MESH,
        ).start()

    def add_partial(n):
        wait_bytes(pi_s.at[n], pr_sem.at[n])
        some = pl.ds(base + 2 * (n % 2), 2)
        mq_s[n // 2, some] = (po_s[n].astype(F32) + pi_s[n].astype(F32)).astype(BF)
        hand_over(n)

    def pass_whole():
        wait_bytes(mq_s.at[1, base + 3 - y], pr_sem.at[3])
        hand_over(3)

    def sum_route(n, device):
        copy = pltpu.make_async_remote_copy(
            dr_s.at[2 * n], dr_s.at[2 * n + 1], ds_sem.at[n], dr_sem.at[n],
            device_id=(f, device), device_id_type=MESH,
        )
        copy.start()
        return copy

    get_one(0)
    get_rest(0)
    middle(0)
    for k in range(4):
        for_mate(0, k)
    get_one(1)
    for k in range(4):
        returned(0, k)
    get_rest(1)
    middle(1)
    for k in range(4):
        for_mate(1, k)
    for_other()
    returned(1, 1)
    returned(1, 2)
    share_partial(0)
    prod = dot_nt(dout_v[:, 0:W], u_s[0]) + dot_nt(dout_v[:, W : 2 * W], u_s[1])
    lax.fori_loop(0, NP, grads, 0)
    both_chips()
    share_partial(1)
    prod = prod + dot_nt(dout_v[:, 2 * W : 3 * W], u_s[2]) + dot_nt(dout_v[:, 3 * W :], u_s[3])
    kept = jnp.where(et_s[...] > 0, prod, 0.0)
    hi = kept.astype(BF)
    lo = (kept - hi.astype(F32)).astype(BF)
    group = jnp.where(over_cap(iota((ROWS, 128), 0)) == iota((ROWS, 128), 1), 1.0, 0.0).astype(BF)
    dr_s[0] = dot(hi, group) + dot(lo, group)
    route = sum_route(0, other)
    add_partial(0)
    lax.fori_loop(NP, 2 * NP, grads, 0)
    share_partial(2)
    add_partial(1)
    route.wait()
    dr_s[2] = dr_s[0] + dr_s[1]
    route = sum_route(1, mate)
    share_whole()
    add_partial(2)
    route.wait()
    total = (dr_s[2] + dr_s[3]).T
    for k in range(top):
        hit = ids_s[k : k + 1, :] == expert
        droute_ref[k : k + 1, :] = jnp.sum(jnp.where(hit, total, 0.0), axis=0, keepdims=True)
    pass_whole()
    for n in range(4):
        wait_bytes(mq_s.at[n // 2, pl.ds(far + 2 * (n % 2), 2)], mr_sem.at[n])

    for h in range(2):
        wait_bytes(sq_s.at[h, pl.ds(0, SRC - 1)], ssem.at[h])
        wait_bytes(sb_s.at[h, pl.ds(0, SRC - 1)], ssem.at[2 + h])
        wait_bytes(xg_s.at[0, 0], qs_sem.at[h])
    for n in range(8):
        wait_bytes(xg_s.at[0, 0], fs_sem.at[n])
        wait_bytes(xo_s.at[n], xs_sem.at[n])
    for t in range(7):
        wait_bytes(sr_s.at[t, pl.ds(0, SRC - 1)], s2_sem.at[t])
    wait_bytes(yo_s, ys_sem)
    for n in range(3):
        wait_bytes(po_s.at[n], ps_sem.at[n])
    wait_bytes(mq_s.at[1, 0], ps_sem.at[3])
    for n in range(4):
        wait_bytes(mq_s.at[n // 2, pl.ds(0, 2)], ms_sem.at[n])


def store_kernel(
    mq_ref, droute_ref, gu_ref, dn_ref,
    moe_hbm, dtok_hbm, out_ref, dgate_hbm, dup_hbm, ddown_hbm, sem,
):
    copies = []
    for j in range(2 * NP):
        cols = pl.ds(j * W, W)
        copies += [
            (gu_ref.at[j, :, pl.ds(0, FH)], dgate_hbm.at[0, cols, :]),
            (gu_ref.at[j, :, pl.ds(FH, FH)], dup_hbm.at[0, cols, :]),
            (dn_ref.at[j], ddown_hbm.at[0, :, cols]),
        ]
    for a, out_hbm in enumerate((moe_hbm, dtok_hbm)):
        for n in range(2 * NP):
            copies.append((mq_ref.at[a, n], out_hbm.at[:, pl.ds(n * W, W)]))
    copies = [pltpu.make_async_copy(s, d, sem.at[n]) for n, (s, d) in enumerate(copies)]
    for one in copies:
        one.start()
    out_ref[...] = droute_ref[...]
    for one in copies:
        one.wait()


def per_device(tokens, expert_ids, route_weights, d_out, gate_weight, up_weight, down_weight):
    hbm = pl.BlockSpec(memory_space=pl.ANY)
    vmem = pl.BlockSpec(memory_space=pltpu.VMEM)
    shape = jax.ShapeDtypeStruct
    dma = pltpu.SemaphoreType.DMA
    v = pltpu.VMEM
    top = route_weights.shape[1]
    mq, droute, gu, dn = pl.pallas_call(
        kernel,
        out_shape=(
            v((2, 2 * NP, TOK, W), BF), v((top, TOK), F32),
            v((2 * NP, W, 2 * FH), BF), v((2 * NP, FH, W), BF),
        ),
        in_specs=[hbm] * 7,
        out_specs=(vmem, vmem, vmem, vmem),
        scratch_shapes=[
            v((top, TOK), jnp.int32), v((top, TOK), F32),
            v((TOK, HALF), BF), v((TOK, HALF), BF),
            v((ROWS, TOK), BF), v((ROWS, 128), F32),
            v((TOK, ROWS), BF), v((TOK, ROWS), BF), v((TOK, ROWS), BF),
            v((ROWS, 2 * W), F32),
            v((2, SRC, MSG, Q), BF), v((2, SRC, MSG, Q), BF),
            v((2, SRC, 2 * MSG, Q), BF), v((2, SRC, 2 * MSG, Q), BF),
            v((2 * NP, 2, ROWS, W), BF),
            v((ROWS, 2 * FH), F32), v((ROWS, FH), F32),
            v((ROWS, FH), BF), v((ROWS, 2 * FH), BF),
            v((8, ROWS, W), BF), v((8, ROWS, W), BF),
            v((ROWS, W), BF), v((ROWS, W), BF), v((ROWS, W), F32), v((ROWS, W), F32),
            v((7, SRC, MSG, Q), BF), v((7, SRC, MSG, Q), BF),
            v((7, ROWS, W), BF),
            v((3, 2, TOK, W), BF), v((3, 2, TOK, W), BF),
            v((4, TOK, 128), F32),
            pltpu.SemaphoreType.REGULAR((2,)),
            dma((4,)), dma((2,)), dma((4,)), dma((4,)), dma((4,)), dma((8,)), dma((8,)), dma((2,)), dma((2,)),
            dma((8,)), dma((8,)), dma, dma, dma((7,)), dma((7,)), dma((7,)),
            dma((4,)), dma((4,)), dma((4,)), dma((4,)), dma((2,)), dma((2,)),
        ],
        compiler_params=pltpu.CompilerParams(
            collective_id=0, has_side_effects=True, vmem_limit_bytes=46 * 1024 * 1024
        ),
        cost_estimate=pl.CostEstimate(flops=11_000_000_000, bytes_accessed=12_000_000, transcendentals=200_000),
    )(expert_ids.T, route_weights.T, tokens, d_out, gate_weight, up_weight, down_weight)
    moe, dtok, droute, dgate, dup, ddown = pl.pallas_call(
        store_kernel,
        out_shape=(
            shape((TOK, D), BF), shape((TOK, D), BF), shape((top, TOK), F32),
            shape(gate_weight.shape, BF), shape(up_weight.shape, BF), shape(down_weight.shape, BF),
        ),
        in_specs=[vmem, vmem, vmem, vmem],
        out_specs=(hbm, hbm, vmem, hbm, hbm, hbm),
        scratch_shapes=[dma((10 * NP,))],
        compiler_params=pltpu.CompilerParams(vmem_limit_bytes=1024 * 1024),
        cost_estimate=pl.CostEstimate(flops=0, bytes_accessed=12_000_000, transcendentals=0),
    )(mq, droute, gu, dn)
    return moe, dtok, droute.T, dgate, dup, ddown


def solution(mesh):
    in_specs = (
        P("fsdp", None),
        P("fsdp", None),
        P("fsdp", None),
        P("fsdp", None),
        P("fsdp", None, "expert"),
        P("fsdp", None, "expert"),
        P("fsdp", "expert", None),
    )
    out_specs = (
        P("fsdp", None),
        P("fsdp", None),
        P("fsdp", None),
        P("fsdp", None, "expert"),
        P("fsdp", None, "expert"),
        P("fsdp", "expert", None),
    )
    return jax.shard_map(
        per_device, mesh=mesh, in_specs=in_specs, out_specs=out_specs, check_vma=False
    )
```

```python
import jax
import jax.numpy as jnp
from jax import lax
from jax.experimental import pallas as pl
from jax.experimental.pallas import tpu as pltpu
from jax.sharding import PartitionSpec as P

MESH = pl.DeviceIdType.MESH
BF = jnp.bfloat16
F32 = jnp.float32

D = 4096
FH = 384
SRC = 32
TOK = 128
CAP = 12
ROWS = SRC * CAP
W = 512
MSG = 4 * CAP
Q = W // 4
HALF = D // 2
NP = HALF // W


def dot(a, b):
    return lax.dot_general(a, b, (((1,), (0,)), ((), ())), preferred_element_type=F32)


def dot_nt(a, b):
    return lax.dot_general(a, b, (((1,), (1,)), ((), ())), preferred_element_type=F32)


def dot_tn(a, b):
    return lax.dot_general(a, b, (((0,), (0,)), ((), ())), preferred_element_type=F32)


def iota(shape, dim):
    return lax.broadcasted_iota(jnp.int32, shape, dim)


def over_cap(j):
    return (j * 5462) >> 16


def to_message(rows, s):
    some = slice(s * CAP, (s + 1) * CAP)
    return jnp.concatenate([rows[some, q * Q : (q + 1) * Q] for q in range(4)], axis=0)


def from_messages(msgs, q):
    return jnp.concatenate([msgs[s, q * CAP : (q + 1) * CAP, :] for s in range(4)], axis=0)


def step_from(f, dz, dx, dy):
    z, x, y = lax.div(f, 8), lax.rem(lax.div(f, 2), 4), lax.rem(f, 2)
    return lax.rem(z + dz, 4) * 8 + lax.rem(x + dx, 4) * 2 + lax.rem(y + dy, 2)


def spread(i, f):
    a, b, c = lax.rem(i, 4), lax.rem(lax.div(i, 4), 4), lax.div(i, 16)
    return step_from(f, a, lax.rem(a + b, 4), lax.rem(a + b + c, 2))


def wait_bytes(ref, sem):
    pltpu.make_async_copy(ref, ref, sem).wait()


def kernel(
    ids_hbm, w_hbm, tok_hbm, dout_hbm, gate_hbm, up_hbm, down_hbm,
    mq_s, droute_ref, gu_s, dn_s,
    ids_s, w_s, tok_v, dout_v, e_s, gs_s, et_s, whi_s, wlo_s, t_s,
    sq_s, rq_s, sb_s, rb_s, xg_s, gu_acc, dh_acc, hid_s, dgu_s,
    xo_s, xi_s, yo_s, yi_s, v_s, vq_s, sr_s, rr_s, u_s, po_s, pi_s, dr_s,
    round_sem, tok_sem, w_sem, ssem, rsem, lsem, fs_sem, fr_sem, qs_sem, qr_sem,
    xs_sem, xr_sem, ys_sem, yr_sem, s2_sem, r2_sem, l2_sem,
    ps_sem, pr_sem, ms_sem, mr_sem, ds_sem, dr_sem,
):
    f = lax.axis_index("fsdp")
    e = lax.axis_index("expert")
    y, c = lax.div(e, 2), lax.rem(e, 2)
    mate = e + 1 - 2 * c
    other = lax.rem(e + 2, 4)

    bar = pltpu.get_barrier_semaphore()
    x_line = [(step_from(f, 0, n, 0), e) for n in (1, 3, 2)]
    z_line = [(step_from(f, n, 0, 0), e) for n in (1, 3, 2)]
    y_line = [(f, other), (step_from(f, 0, 0, 1), other), (step_from(f, 0, 0, 1), e)]

    def signal(sem, devices):
        for d in devices:
            pl.semaphore_signal(sem, inc=1, device_id=d, device_id_type=MESH)

    signal(bar, z_line + x_line + y_line + [(f, mate)])

    ids_in = pltpu.make_async_copy(ids_hbm, ids_s, tok_sem.at[2])
    w_in = pltpu.make_async_copy(w_hbm, w_s, tok_sem.at[3])
    ids_in.start()
    w_in.start()
    half = pl.ds(pl.multiple_of(c * HALF, HALF), HALF)
    tok_in = pltpu.make_async_copy(tok_hbm.at[:, half], tok_v, tok_sem.at[0])
    dout_in = pltpu.make_async_copy(dout_hbm.at[:, half], dout_v, tok_sem.at[1])
    tok_in.start()
    dout_in.start()

    ids_in.wait()
    w_in.wait()
    top = ids_s.shape[0]
    expert = iota((128, TOK), 0)
    named = jnp.zeros((128, TOK), F32)
    wmat = jnp.zeros((128, TOK), F32)
    for k in range(top):
        hit = ids_s[k : k + 1, :] == expert
        named = named + jnp.where(hit, 1.0, 0.0)
        wmat = wmat + jnp.where(hit, w_s[k : k + 1, :], 0.0)
    earlier = jnp.where(expert < iota((128, TOK), 1), 1.0, 0.0).astype(BF)
    code = jnp.where(named > 0.5, dot(named.astype(BF), earlier) + 1.0, 0.0)
    w_hi = wmat.astype(BF)
    w_mid = (wmat - w_hi.astype(F32)).astype(BF)
    w_lo = (wmat - w_hi.astype(F32) - w_mid.astype(F32)).astype(BF)

    slot = iota((ROWS, 128), 0)
    owner = over_cap(slot)
    rep = jnp.where(owner == iota((ROWS, 128), 1), 1.0, 0.0).astype(BF)
    fills = dot(rep, code.astype(BF)) == (slot - CAP * owner + 1).astype(F32)
    e_s[...] = jnp.where(fills, 1.0, 0.0).astype(BF)
    scale = (dot(rep, w_hi) + dot(rep, w_mid)) + dot(rep, w_lo)
    scale = jnp.sum(jnp.where(fills, scale, 0.0), axis=1, keepdims=True)
    gs_s[...] = jnp.broadcast_to(scale, (ROWS, 128))

    def rows_of(h, piece, at):
        for n in range(2):
            cols = pl.ds(pl.multiple_of(piece * W + n * 256, 256), 256)
            here = at * W + n * 256
            if h == 0:
                t_s[:, here : here + 256] = dot(e_s[...], tok_v[:, cols])
            else:
                cot = dot(e_s[...], dout_v[:, cols])
                for m in range(2):
                    t_s[:, here + m * Q : here + (m + 1) * Q] = cot[:, m * Q : (m + 1) * Q] * gs_s[...]

    def pack_one(h):
        for at in range(2):
            rows_of(h, 2 + lax.rem(y + f + at, 2), at)

        def some_rows(g, carry):
            rows = pl.ds(pl.multiple_of(g * MSG, MSG), MSG)
            for s in range(4):
                some = t_s[rows, (s % 2) * W : (s % 2 + 1) * W]
                sq_s[h, g * 4 + s] = to_message(some, s).astype(BF)
            return carry

        lax.fori_loop(0, SRC // 4, some_rows, 0)

    def pack_two(h):
        for at in range(2):
            rows_of(h, at, at)

        def some_rows(g, carry):
            rows = pl.ds(pl.multiple_of(g * MSG, MSG), MSG)
            for at in range(2):
                some = t_s[rows, at * W : (at + 1) * W]
                for s in range(4):
                    sb_s[h, g * 4 + s, at * MSG : (at + 1) * MSG, :] = to_message(some, s).astype(BF)
            return carry

        lax.fori_loop(0, SRC // 4, some_rows, 0)

    def crossed(f2):
        return lax.rem(e + 2 * lax.rem(f + f2, 2), 4)

    def send_one(h, f2):
        pltpu.make_async_remote_copy(
            sq_s.at[h, f2], rq_s.at[h, f], ssem.at[h], rsem.at[h],
            device_id=(f2, crossed(f2)), device_id_type=MESH,
        ).start()

    def send_two(h, f2):
        pltpu.make_async_remote_copy(
            sb_s.at[h, f2], rb_s.at[h, f], ssem.at[2 + h], rsem.at[2 + h],
            device_id=(f2, crossed(f2)), device_id_type=MESH,
        ).start()

    def to_line(send, h):
        def one(n, carry):
            send(h, step_from(f, n, 0, 0))
            send(h, step_from(f, 0, n, 0))
            return carry

        lax.fori_loop(1, 4, one, 0)
        send(h, step_from(f, 0, 0, 1))

    def to_plane(send, h):
        def one(n, carry):
            a, b = lax.div(n, 3), lax.rem(n, 3)
            send(h, step_from(f, 1 + a, 1 + lax.rem(a + b, 3), 0))
            return carry

        lax.fori_loop(0, 9, one, 0)

    def to_rest(send, h):
        def one(n, carry):
            a, b = lax.rem(n, 4), lax.div(n, 4)
            send(h, step_from(f, a, lax.rem(a + b, 4), 1))
            return carry

        lax.fori_loop(1, 16, one, 0)

    def to_all(send, h):
        def one(n, carry):
            send(h, spread(n, f))
            return carry

        lax.fori_loop(1, SRC, one, 0)

    def one_sent(h):
        wait_bytes(sq_s.at[h, pl.ds(0, SRC - 1)], ssem.at[h])

    def two_sent(h):
        wait_bytes(sb_s.at[h, pl.ds(0, SRC - 1)], ssem.at[2 + h])

    def keep(h):
        pltpu.make_async_copy(sq_s.at[h, f], rq_s.at[h, f], lsem.at[h]).start()

    def keep_two(h):
        pltpu.make_async_copy(sb_s.at[h, f], rb_s.at[h, f], lsem.at[2 + h]).start()

    tok_in.wait()
    pack_one(0)
    pl.semaphore_wait(bar, 10)
    signal(round_sem.at[0], x_line)
    to_line(send_one, 0)
    dout_in.wait()
    pack_one(1)
    pl.semaphore_wait(round_sem.at[0], 3)
    signal(round_sem.at[1], y_line)
    to_plane(send_one, 0)
    to_line(send_one, 1)
    pack_two(0)
    pl.semaphore_wait(round_sem.at[1], 3)
    to_rest(send_one, 0)
    to_plane(send_one, 1)
    keep(0)
    one_sent(0)
    to_rest(send_one, 1)
    keep(1)
    one_sent(1)
    to_all(send_two, 0)
    for j in range(2 * NP):
        cols = pl.ds(j * W, W)
        pltpu.make_async_copy(gate_hbm.at[0, cols, :], gu_s.at[j, :, pl.ds(0, FH)], w_sem.at[0]).start()
        pltpu.make_async_copy(up_hbm.at[0, cols, :], gu_s.at[j, :, pl.ds(FH, FH)], w_sem.at[0]).start()
        pltpu.make_async_copy(down_hbm.at[0, :, cols], dn_s.at[j], w_sem.at[1]).start()

    def first(h, j):
        if h == 1:
            dh_acc[...] += dot_nt(xg_s[j, 1], dn_s[j])
            return
        for n in range(3):
            cols = slice(n * 256, (n + 1) * 256)
            gu_acc[:, cols] += dot(xg_s[j, 0], gu_s[j, :, cols])

    order = (2 + y, 0, 1, 3 - y)
    base = c * NP
    far = (1 - c) * NP

    def unpack(h, msgs, n, pieces):
        wait_bytes(msgs.at[h, pl.ds(0, SRC - 1)], rsem.at[2 * n + h])
        sent = (sq_s, sb_s)[n]
        pltpu.make_async_copy(sent.at[h, f], msgs.at[h, f], lsem.at[2 * n + h]).wait()

        def some_rows(g, carry):
            rows = pl.ds(pl.multiple_of(g * MSG, MSG), MSG)
            some = msgs[h, pl.ds(g * 4, 4)].astype(F32)
            for at, piece in enumerate(pieces):
                part = some[:, at * MSG : (at + 1) * MSG, :]
                for q in range(4):
                    xg_s[base + piece, h, rows, q * Q : (q + 1) * Q] = from_messages(part, q).astype(BF)
            return carry

        lax.fori_loop(0, SRC // 4, some_rows, 0)

    def to_mate(h, k):
        j = base + order[k]
        pltpu.make_async_remote_copy(
            xg_s.at[j, h], xg_s.at[j, h], fs_sem.at[4 * h + k], fr_sem.at[4 * h + k],
            device_id=(f, mate), device_id_type=MESH,
        ).start()

    def from_mate(h, k):
        j = far + order[k]
        wait_bytes(xg_s.at[j, h], fr_sem.at[4 * h + k])
        first(h, j)

    def get_one(h):
        j = base + order[0]
        unpack(h, rq_s, 0, order[0:1])
        pltpu.make_async_remote_copy(
            xg_s.at[j, h], xg_s.at[j, h], qs_sem.at[h], qr_sem.at[h],
            device_id=(f, other), device_id_type=MESH,
        ).start()
        to_mate(h, 0)

    def use_one(h):
        first(h, base + order[0])
        from_mate(h, 0)

    def get_rest(h):
        unpack(h, rb_s, 1, order[1:3])
        to_mate(h, 1)
        to_mate(h, 2)
        first(h, base + order[1])
        first(h, base + order[2])
        there = base + order[3]
        wait_bytes(xg_s.at[there, h], qr_sem.at[h])
        to_mate(h, 3)
        first(h, there)
        for k in range(1, 4):
            from_mate(h, k)

    def middle(h):
        def some_rows(n, carry):
            rows = pl.ds(pl.multiple_of(n * 96, 96), 96)
            gate = gu_acc[rows, 0:FH]
            up = gu_acc[rows, FH : 2 * FH]
            sig = jax.nn.sigmoid(gate)
            act = gate * sig
            if h == 0:
                hid_s[rows, :] = (act * up).astype(BF)
                return carry
            dh = dh_acc[rows, :]
            slope = sig * (1.0 + gate * (1.0 - sig))
            dgu_s[rows, 0:FH] = (dh * up * slope).astype(BF)
            dgu_s[rows, FH : 2 * FH] = (dh * act).astype(BF)
            return carry

        lax.fori_loop(0, ROWS // 96, some_rows, 0)

    back = ((0, 1, 2, 3), (3 - y, 0, 1, 2 + y))

    def second(a, j):
        if a == 0:
            return dot(hid_s[...], dn_s[j])
        return dot_nt(dgu_s[...], gu_s[j])

    def for_mate(a, k):
        t = 4 * a + k
        xo_s[t] = second(a, far + back[a][k]).astype(BF)
        pltpu.make_async_remote_copy(
            xo_s.at[t], xi_s.at[t], xs_sem.at[t], xr_sem.at[t],
            device_id=(f, mate), device_id_type=MESH,
        ).start()

    def chip_sum(a, k):
        t = 4 * a + k
        own = second(a, base + back[a][k])
        wait_bytes(xi_s.at[t], xr_sem.at[t])
        return own + xi_s[t].astype(F32)

    def send_back(t):
        def some_rows(g, carry):
            some = v_s[pl.ds(pl.multiple_of(g * MSG, MSG), MSG), :]
            for s in range(4):
                sr_s[t, g * 4 + s] = to_message(some, s).astype(BF)
            return carry

        lax.fori_loop(0, SRC // 4, some_rows, 0)

        def one(i, carry):
            f2 = spread(i, f)
            pltpu.make_async_remote_copy(
                sr_s.at[t, f2], rr_s.at[t, f], s2_sem.at[t], r2_sem.at[t],
                device_id=(f2, crossed(f2)), device_id_type=MESH,
            ).start()
            return carry

        lax.fori_loop(1, SRC, one, 0)
        pltpu.make_async_copy(sr_s.at[t, f], rr_s.at[t, f], l2_sem.at[t]).start()

    def returned(a, k):
        v_s[...] = chip_sum(a, k)
        send_back(3 * a + k)

    def for_other():
        same = lax.rem(over_cap(iota((ROWS, W), 0)) + f, 2) == 0
        a, b = chip_sum(1, 0), chip_sum(1, 3)
        yo_s[...] = jnp.where(same, a, b).astype(BF)
        vq_s[...] = jnp.where(same, b, a)
        pltpu.make_async_remote_copy(
            yo_s, yi_s, ys_sem, yr_sem, device_id=(f, other), device_id_type=MESH
        ).start()

    def both_chips():
        wait_bytes(yi_s, yr_sem)
        v_s[...] = vq_s[...] + yi_s[...].astype(F32)
        send_back(6)

    def grads(j, carry):
        for n in range(3):
            some = slice(n * 256, (n + 1) * 256)
            gu_s[j, :, some] = dot_tn(xg_s[j, 0], dgu_s[:, some]).astype(BF)
        dn_s[j] = dot_tn(hid_s[...], xg_s[j, 1]).astype(BF)
        return carry

    def landed(t):
        wait_bytes(rr_s.at[t, pl.ds(0, SRC - 1)], r2_sem.at[t])
        pltpu.make_async_copy(sr_s.at[t, f], rr_s.at[t, f], l2_sem.at[t]).wait()

        def some_rows(g, carry):
            rows = pl.ds(pl.multiple_of(g * MSG, MSG), MSG)
            msgs = rr_s[t, pl.ds(g * 4, 4)].astype(F32)
            for q in range(4):
                u_s[t, rows, q * Q : (q + 1) * Q] = from_messages(msgs, q).astype(BF)
            return carry

        lax.fori_loop(0, SRC // 4, some_rows, 0)

    def combined(t):
        u = u_s[t]
        if t >= 4:
            return dot(et_s[...], u).astype(BF)
        return (dot(whi_s[...], u) + dot(wlo_s[...], u)).astype(BF)

    def share_partial(n):
        for k in range(2):
            landed(2 * n + k)
            po_s[n, k] = combined(2 * n + k)
        pltpu.make_async_remote_copy(
            po_s.at[n], pi_s.at[n], ps_sem.at[n], pr_sem.at[n],
            device_id=(f, other), device_id_type=MESH,
        ).start()

    def share_whole():
        n = base + 2 + y
        landed(6)
        mq_s[1, n] = combined(6)
        pltpu.make_async_remote_copy(
            mq_s.at[1, n], mq_s.at[1, n], ps_sem.at[3], pr_sem.at[3],
            device_id=(f, other), device_id_type=MESH,
        ).start()

    def hand_over(n):
        some = pl.ds(base + 2 * (n % 2), 2)
        pltpu.make_async_remote_copy(
            mq_s.at[n // 2, some], mq_s.at[n // 2, some], ms_sem.at[n], mr_sem.at[n],
            device_id=(f, mate), device_id_type=MESH,
        ).start()

    def add_partial(n):
        wait_bytes(pi_s.at[n], pr_sem.at[n])
        some = pl.ds(base + 2 * (n % 2), 2)
        mq_s[n // 2, some] = (po_s[n].astype(F32) + pi_s[n].astype(F32)).astype(BF)
        hand_over(n)

    def pass_whole():
        wait_bytes(mq_s.at[1, base + 3 - y], pr_sem.at[3])
        hand_over(3)

    def sum_route(n, device):
        copy = pltpu.make_async_remote_copy(
            dr_s.at[2 * n], dr_s.at[2 * n + 1], ds_sem.at[n], dr_sem.at[n],
            device_id=(f, device), device_id_type=MESH,
        )
        copy.start()
        return copy

    get_one(0)
    keep_two(0)
    pack_two(1)
    get_one(1)
    keep_two(1)

    gu_acc[...] = jnp.zeros_like(gu_acc)
    dh_acc[...] = jnp.zeros_like(dh_acc)
    slot_t = iota((TOK, ROWS), 1)
    owner_t = over_cap(slot_t)
    rep_t = jnp.where(owner_t == iota((TOK, ROWS), 0), 1.0, 0.0).astype(BF)
    fills_t = dot(code.T.astype(BF), rep_t) == (slot_t - CAP * owner_t + 1).astype(F32)
    et_s[...] = jnp.where(fills_t, 1.0, 0.0).astype(BF)
    wmat_t = wmat.T
    w_hi_t = wmat_t.astype(BF)
    w_lo_t = (wmat_t - w_hi_t.astype(F32)).astype(BF)
    whi_s[...] = jnp.where(fills_t, dot(w_hi_t, rep_t), 0.0).astype(BF)
    wlo_s[...] = jnp.where(fills_t, dot(w_lo_t, rep_t), 0.0).astype(BF)
    wait_bytes(gu_s, w_sem.at[0])
    wait_bytes(dn_s, w_sem.at[1])

    use_one(0)
    use_one(1)
    two_sent(0)
    to_all(send_two, 1)
    get_rest(0)
    middle(0)
    for k in range(4):
        for_mate(0, k)
    for k in range(3):
        returned(0, k)
    get_rest(1)
    middle(1)
    for k in range(4):
        for_mate(1, k)
    for_other()
    returned(0, 3)
    returned(1, 1)
    returned(1, 2)
    share_partial(0)
    both_chips()
    share_partial(1)
    lax.fori_loop(0, NP, grads, 0)
    share_partial(2)
    prod = dot_nt(dout_v[:, 0:W], u_s[0])
    for k in range(1, 4):
        prod = prod + dot_nt(dout_v[:, k * W : (k + 1) * W], u_s[k])
    kept = jnp.where(et_s[...] > 0, prod, 0.0)
    hi = kept.astype(BF)
    lo = (kept - hi.astype(F32)).astype(BF)
    group = jnp.where(over_cap(iota((ROWS, 128), 0)) == iota((ROWS, 128), 1), 1.0, 0.0).astype(BF)
    dr_s[0] = dot(hi, group) + dot(lo, group)
    route = sum_route(0, other)
    add_partial(0)
    lax.fori_loop(NP, 2 * NP, grads, 0)
    add_partial(1)
    share_whole()
    route.wait()
    dr_s[2] = dr_s[0] + dr_s[1]
    route = sum_route(1, mate)
    add_partial(2)
    route.wait()
    total = (dr_s[2] + dr_s[3]).T
    for k in range(top):
        hit = ids_s[k : k + 1, :] == expert
        droute_ref[k : k + 1, :] = jnp.sum(jnp.where(hit, total, 0.0), axis=0, keepdims=True)
    pass_whole()
    for n in range(4):
        wait_bytes(mq_s.at[n // 2, pl.ds(far + 2 * (n % 2), 2)], mr_sem.at[n])

    two_sent(1)
    for h in range(2):
        wait_bytes(xg_s.at[0, 0], qs_sem.at[h])
    for n in range(8):
        wait_bytes(xg_s.at[0, 0], fs_sem.at[n])
        wait_bytes(xo_s.at[n], xs_sem.at[n])
    for t in range(7):
        wait_bytes(sr_s.at[t, pl.ds(0, SRC - 1)], s2_sem.at[t])
    wait_bytes(yo_s, ys_sem)
    for n in range(3):
        wait_bytes(po_s.at[n], ps_sem.at[n])
    wait_bytes(mq_s.at[1, 0], ps_sem.at[3])
    for n in range(4):
        wait_bytes(mq_s.at[n // 2, pl.ds(0, 2)], ms_sem.at[n])


def store_kernel(
    mq_ref, droute_ref, gu_ref, dn_ref,
    moe_hbm, dtok_hbm, out_ref, dgate_hbm, dup_hbm, ddown_hbm, sem,
):
    copies = []
    for j in range(2 * NP):
        cols = pl.ds(j * W, W)
        copies += [
            (gu_ref.at[j, :, pl.ds(0, FH)], dgate_hbm.at[0, cols, :]),
            (gu_ref.at[j, :, pl.ds(FH, FH)], dup_hbm.at[0, cols, :]),
            (dn_ref.at[j], ddown_hbm.at[0, :, cols]),
        ]
    for a, out_hbm in enumerate((moe_hbm, dtok_hbm)):
        for n in range(2 * NP):
            copies.append((mq_ref.at[a, n], out_hbm.at[:, pl.ds(n * W, W)]))
    copies = [pltpu.make_async_copy(s, d, sem.at[n]) for n, (s, d) in enumerate(copies)]
    for one in copies:
        one.start()
    out_ref[...] = droute_ref[...]
    for one in copies:
        one.wait()


def per_device(tokens, expert_ids, route_weights, d_out, gate_weight, up_weight, down_weight):
    hbm = pl.BlockSpec(memory_space=pl.ANY)
    vmem = pl.BlockSpec(memory_space=pltpu.VMEM)
    shape = jax.ShapeDtypeStruct
    dma = pltpu.SemaphoreType.DMA
    v = pltpu.VMEM
    top = route_weights.shape[1]
    mq, droute, gu, dn = pl.pallas_call(
        kernel,
        out_shape=(
            v((2, 2 * NP, TOK, W), BF), v((top, TOK), F32),
            v((2 * NP, W, 2 * FH), BF), v((2 * NP, FH, W), BF),
        ),
        in_specs=[hbm] * 7,
        out_specs=(vmem, vmem, vmem, vmem),
        scratch_shapes=[
            v((top, TOK), jnp.int32), v((top, TOK), F32),
            v((TOK, HALF), BF), v((TOK, HALF), BF),
            v((ROWS, TOK), BF), v((ROWS, 128), F32),
            v((TOK, ROWS), BF), v((TOK, ROWS), BF), v((TOK, ROWS), BF),
            v((ROWS, 2 * W), F32),
            v((2, SRC, MSG, Q), BF), v((2, SRC, MSG, Q), BF),
            v((2, SRC, 2 * MSG, Q), BF), v((2, SRC, 2 * MSG, Q), BF),
            v((2 * NP, 2, ROWS, W), BF),
            v((ROWS, 2 * FH), F32), v((ROWS, FH), F32),
            v((ROWS, FH), BF), v((ROWS, 2 * FH), BF),
            v((8, ROWS, W), BF), v((8, ROWS, W), BF),
            v((ROWS, W), BF), v((ROWS, W), BF), v((ROWS, W), F32), v((ROWS, W), F32),
            v((7, SRC, MSG, Q), BF), v((7, SRC, MSG, Q), BF),
            v((7, ROWS, W), BF),
            v((3, 2, TOK, W), BF), v((3, 2, TOK, W), BF),
            v((4, TOK, 128), F32),
            pltpu.SemaphoreType.REGULAR((2,)),
            dma((4,)), dma((2,)), dma((4,)), dma((4,)), dma((4,)), dma((8,)), dma((8,)), dma((2,)), dma((2,)),
            dma((8,)), dma((8,)), dma, dma, dma((7,)), dma((7,)), dma((7,)),
            dma((4,)), dma((4,)), dma((4,)), dma((4,)), dma((2,)), dma((2,)),
        ],
        compiler_params=pltpu.CompilerParams(
            collective_id=0, has_side_effects=True, vmem_limit_bytes=46 * 1024 * 1024
        ),
        cost_estimate=pl.CostEstimate(flops=11_000_000_000, bytes_accessed=12_000_000, transcendentals=200_000),
    )(expert_ids.T, route_weights.T, tokens, d_out, gate_weight, up_weight, down_weight)
    moe, dtok, droute, dgate, dup, ddown = pl.pallas_call(
        store_kernel,
        out_shape=(
            shape((TOK, D), BF), shape((TOK, D), BF), shape((top, TOK), F32),
            shape(gate_weight.shape, BF), shape(up_weight.shape, BF), shape(down_weight.shape, BF),
        ),
        in_specs=[vmem, vmem, vmem, vmem],
        out_specs=(hbm, hbm, vmem, hbm, hbm, hbm),
        scratch_shapes=[dma((10 * NP,))],
        compiler_params=pltpu.CompilerParams(vmem_limit_bytes=1024 * 1024),
        cost_estimate=pl.CostEstimate(flops=0, bytes_accessed=12_000_000, transcendentals=0),
    )(mq, droute, gu, dn)
    return moe, dtok, droute.T, dgate, dup, ddown


def solution(mesh):
    in_specs = (
        P("fsdp", None),
        P("fsdp", None),
        P("fsdp", None),
        P("fsdp", None),
        P("fsdp", None, "expert"),
        P("fsdp", None, "expert"),
        P("fsdp", "expert", None),
    )
    out_specs = (
        P("fsdp", None),
        P("fsdp", None),
        P("fsdp", None),
        P("fsdp", None, "expert"),
        P("fsdp", None, "expert"),
        P("fsdp", "expert", None),
    )
    return jax.shard_map(
        per_device, mesh=mesh, in_specs=in_specs, out_specs=out_specs, check_vma=False
    )
```

```python
import jax
import jax.numpy as jnp
from jax import lax
from jax.experimental import pallas as pl
from jax.experimental.pallas import tpu as pltpu
from jax.sharding import PartitionSpec as P

MESH = pl.DeviceIdType.MESH
BF = jnp.bfloat16
F32 = jnp.float32

D = 4096
FH = 384
SRC = 32
TOK = 128
CAP = 12
ROWS = SRC * CAP
W = 512
MSG = 4 * CAP
Q = W // 4
HALF = D // 2
NP = HALF // W


def dot(a, b):
    return lax.dot_general(a, b, (((1,), (0,)), ((), ())), preferred_element_type=F32)


def dot_nt(a, b):
    return lax.dot_general(a, b, (((1,), (1,)), ((), ())), preferred_element_type=F32)


def dot_tn(a, b):
    return lax.dot_general(a, b, (((0,), (0,)), ((), ())), preferred_element_type=F32)


def iota(shape, dim):
    return lax.broadcasted_iota(jnp.int32, shape, dim)


def over_cap(j):
    return (j * 5462) >> 16


def to_message(rows, s):
    some = slice(s * CAP, (s + 1) * CAP)
    return jnp.concatenate([rows[some, q * Q : (q + 1) * Q] for q in range(4)], axis=0)


def from_messages(msgs, q):
    return jnp.concatenate([msgs[s, q * CAP : (q + 1) * CAP, :] for s in range(4)], axis=0)


def step_from(f, dz, dx, dy):
    z, x, y = lax.div(f, 8), lax.rem(lax.div(f, 2), 4), lax.rem(f, 2)
    return lax.rem(z + dz, 4) * 8 + lax.rem(x + dx, 4) * 2 + lax.rem(y + dy, 2)


def spread(i, f):
    a, b, c = lax.rem(i, 4), lax.rem(lax.div(i, 4), 4), lax.div(i, 16)
    return step_from(f, a, lax.rem(a + b, 4), lax.rem(a + b + c, 2))


def wait_bytes(ref, sem):
    pltpu.make_async_copy(ref, ref, sem).wait()


def kernel(
    ids_hbm, w_hbm, tok_hbm, dout_hbm, gate_hbm, up_hbm, down_hbm,
    mq_s, droute_ref, gu_s, dn_s,
    ids_s, w_s, tok_v, dout_v, e_s, gs_s, et_s, whi_s, wlo_s, t_s,
    sq_s, rq_s, sb_s, rb_s, xg_s, gu_acc, dh_acc, hid_s, dgu_s,
    xo_s, xi_s, yo_s, yi_s, v_s, vq_s, sr_s, rr_s, u_s, po_s, pi_s, dr_s,
    round_sem, tok_sem, w_sem, ssem, rsem, lsem, fs_sem, fr_sem, qs_sem, qr_sem,
    xs_sem, xr_sem, ys_sem, yr_sem, s2_sem, r2_sem, l2_sem,
    ps_sem, pr_sem, ms_sem, mr_sem, ds_sem, dr_sem,
):
    f = lax.axis_index("fsdp")
    e = lax.axis_index("expert")
    y, c = lax.div(e, 2), lax.rem(e, 2)
    mate = e + 1 - 2 * c
    other = lax.rem(e + 2, 4)

    bar = pltpu.get_barrier_semaphore()
    x_line = [(step_from(f, 0, n, 0), e) for n in (1, 3, 2)]
    z_line = [(step_from(f, n, 0, 0), e) for n in (1, 3, 2)]
    y_line = [(f, other), (step_from(f, 0, 0, 1), other), (step_from(f, 0, 0, 1), e)]

    def signal(sem, devices):
        for d in devices:
            pl.semaphore_signal(sem, inc=1, device_id=d, device_id_type=MESH)

    signal(bar, z_line + x_line + y_line + [(f, mate)])

    ids_in = pltpu.make_async_copy(ids_hbm, ids_s, tok_sem.at[2])
    w_in = pltpu.make_async_copy(w_hbm, w_s, tok_sem.at[3])
    ids_in.start()
    w_in.start()
    half = pl.ds(pl.multiple_of(c * HALF, HALF), HALF)
    tok_in = pltpu.make_async_copy(tok_hbm.at[:, half], tok_v, tok_sem.at[0])
    dout_in = pltpu.make_async_copy(dout_hbm.at[:, half], dout_v, tok_sem.at[1])
    tok_in.start()
    dout_in.start()

    ids_in.wait()
    w_in.wait()
    top = ids_s.shape[0]
    expert = iota((128, TOK), 0)
    named = jnp.zeros((128, TOK), F32)
    wmat = jnp.zeros((128, TOK), F32)
    for k in range(top):
        hit = ids_s[k : k + 1, :] == expert
        named = named + jnp.where(hit, 1.0, 0.0)
        wmat = wmat + jnp.where(hit, w_s[k : k + 1, :], 0.0)
    earlier = jnp.where(expert < iota((128, TOK), 1), 1.0, 0.0).astype(BF)
    code = jnp.where(named > 0.5, dot(named.astype(BF), earlier) + 1.0, 0.0)
    w_hi = wmat.astype(BF)
    w_mid = (wmat - w_hi.astype(F32)).astype(BF)
    w_lo = (wmat - w_hi.astype(F32) - w_mid.astype(F32)).astype(BF)

    slot = iota((ROWS, 128), 0)
    owner = over_cap(slot)
    rep = jnp.where(owner == iota((ROWS, 128), 1), 1.0, 0.0).astype(BF)
    fills = dot(rep, code.astype(BF)) == (slot - CAP * owner + 1).astype(F32)
    e_s[...] = jnp.where(fills, 1.0, 0.0).astype(BF)
    scale = (dot(rep, w_hi) + dot(rep, w_mid)) + dot(rep, w_lo)
    scale = jnp.sum(jnp.where(fills, scale, 0.0), axis=1, keepdims=True)
    gs_s[...] = jnp.broadcast_to(scale, (ROWS, 128))

    def rows_of(h, piece, at):
        for n in range(2):
            cols = pl.ds(pl.multiple_of(piece * W + n * 256, 256), 256)
            here = at * W + n * 256
            if h == 0:
                t_s[:, here : here + 256] = dot(e_s[...], tok_v[:, cols])
            else:
                cot = dot(e_s[...], dout_v[:, cols])
                for m in range(2):
                    t_s[:, here + m * Q : here + (m + 1) * Q] = cot[:, m * Q : (m + 1) * Q] * gs_s[...]

    def pack_one(h):
        for at in range(2):
            rows_of(h, 2 + lax.rem(y + f + at, 2), at)

        def some_rows(g, carry):
            rows = pl.ds(pl.multiple_of(g * MSG, MSG), MSG)
            for s in range(4):
                some = t_s[rows, (s % 2) * W : (s % 2 + 1) * W]
                sq_s[h, g * 4 + s] = to_message(some, s).astype(BF)
            return carry

        lax.fori_loop(0, SRC // 4, some_rows, 0)

    def pack_two(h):
        for at in range(2):
            rows_of(h, at, at)

        def some_rows(g, carry):
            rows = pl.ds(pl.multiple_of(g * MSG, MSG), MSG)
            for at in range(2):
                some = t_s[rows, at * W : (at + 1) * W]
                for s in range(4):
                    sb_s[h, g * 4 + s, at * MSG : (at + 1) * MSG, :] = to_message(some, s).astype(BF)
            return carry

        lax.fori_loop(0, SRC // 4, some_rows, 0)

    def crossed(f2):
        return lax.rem(e + 2 * lax.rem(f + f2, 2), 4)

    def send_one(h, f2):
        pltpu.make_async_remote_copy(
            sq_s.at[h, f2], rq_s.at[h, f], ssem.at[h], rsem.at[h],
            device_id=(f2, crossed(f2)), device_id_type=MESH,
        ).start()

    def send_two(h, f2):
        pltpu.make_async_remote_copy(
            sb_s.at[h, f2], rb_s.at[h, f], ssem.at[2 + h], rsem.at[2 + h],
            device_id=(f2, crossed(f2)), device_id_type=MESH,
        ).start()

    def to_line(send, h):
        def one(n, carry):
            send(h, step_from(f, n, 0, 0))
            send(h, step_from(f, 0, n, 0))
            return carry

        lax.fori_loop(1, 4, one, 0)
        send(h, step_from(f, 0, 0, 1))

    def to_plane(send, h):
        def one(n, carry):
            a, b = lax.div(n, 3), lax.rem(n, 3)
            send(h, step_from(f, 1 + a, 1 + lax.rem(a + b, 3), 0))
            return carry

        lax.fori_loop(0, 9, one, 0)

    def to_rest(send, h):
        def one(n, carry):
            a, b = lax.rem(n, 4), lax.div(n, 4)
            send(h, step_from(f, a, lax.rem(a + b, 4), 1))
            return carry

        lax.fori_loop(1, 16, one, 0)

    def to_all(send, h):
        def one(n, carry):
            send(h, spread(n, f))
            return carry

        lax.fori_loop(1, SRC, one, 0)

    def one_sent(h):
        wait_bytes(sq_s.at[h, pl.ds(0, SRC - 1)], ssem.at[h])

    def two_sent(h):
        wait_bytes(sb_s.at[h, pl.ds(0, SRC - 1)], ssem.at[2 + h])

    def keep(h):
        pltpu.make_async_copy(sq_s.at[h, f], rq_s.at[h, f], lsem.at[h]).start()

    def keep_two(h):
        pltpu.make_async_copy(sb_s.at[h, f], rb_s.at[h, f], lsem.at[2 + h]).start()

    tok_in.wait()
    pack_one(0)
    pl.semaphore_wait(bar, 10)
    signal(round_sem.at[0], x_line)
    to_line(send_one, 0)
    dout_in.wait()
    pack_one(1)
    pl.semaphore_wait(round_sem.at[0], 3)
    signal(round_sem.at[1], y_line)
    to_plane(send_one, 0)
    to_line(send_one, 1)
    pack_two(0)
    pl.semaphore_wait(round_sem.at[1], 3)
    to_rest(send_one, 0)
    to_plane(send_one, 1)
    keep(0)
    one_sent(0)
    to_rest(send_one, 1)
    keep(1)
    one_sent(1)
    to_all(send_two, 0)
    for j in range(2 * NP):
        cols = pl.ds(j * W, W)
        pltpu.make_async_copy(gate_hbm.at[0, cols, :], gu_s.at[j, :, pl.ds(0, FH)], w_sem.at[0]).start()
        pltpu.make_async_copy(up_hbm.at[0, cols, :], gu_s.at[j, :, pl.ds(FH, FH)], w_sem.at[0]).start()
        pltpu.make_async_copy(down_hbm.at[0, :, cols], dn_s.at[j], w_sem.at[1]).start()

    def first(h, j):
        if h == 1:
            dh_acc[...] += dot_nt(xg_s[j, 1], dn_s[j])
            return
        for n in range(3):
            cols = slice(n * 256, (n + 1) * 256)
            gu_acc[:, cols] += dot(xg_s[j, 0], gu_s[j, :, cols])

    order = (2 + y, 0, 1, 3 - y)
    base = c * NP
    far = (1 - c) * NP

    def unpack(h, msgs, n, pieces):
        wait_bytes(msgs.at[h, pl.ds(0, SRC - 1)], rsem.at[2 * n + h])
        sent = (sq_s, sb_s)[n]
        pltpu.make_async_copy(sent.at[h, f], msgs.at[h, f], lsem.at[2 * n + h]).wait()

        def some_rows(g, carry):
            rows = pl.ds(pl.multiple_of(g * MSG, MSG), MSG)
            some = msgs[h, pl.ds(g * 4, 4)].astype(F32)
            for at, piece in enumerate(pieces):
                part = some[:, at * MSG : (at + 1) * MSG, :]
                for q in range(4):
                    xg_s[base + piece, h, rows, q * Q : (q + 1) * Q] = from_messages(part, q).astype(BF)
            return carry

        lax.fori_loop(0, SRC // 4, some_rows, 0)

    def to_mate(h, k):
        j = base + order[k]
        pltpu.make_async_remote_copy(
            xg_s.at[j, h], xg_s.at[j, h], fs_sem.at[4 * h + k], fr_sem.at[4 * h + k],
            device_id=(f, mate), device_id_type=MESH,
        ).start()

    def from_mate(h, k):
        j = far + order[k]
        wait_bytes(xg_s.at[j, h], fr_sem.at[4 * h + k])
        first(h, j)

    def get_one(h):
        j = base + order[0]
        unpack(h, rq_s, 0, order[0:1])
        pltpu.make_async_remote_copy(
            xg_s.at[j, h], xg_s.at[j, h], qs_sem.at[h], qr_sem.at[h],
            device_id=(f, other), device_id_type=MESH,
        ).start()
        to_mate(h, 0)

    def use_one(h):
        first(h, base + order[0])
        from_mate(h, 0)

    def get_rest(h):
        unpack(h, rb_s, 1, order[1:3])
        to_mate(h, 1)
        to_mate(h, 2)
        first(h, base + order[1])
        first(h, base + order[2])
        there = base + order[3]
        wait_bytes(xg_s.at[there, h], qr_sem.at[h])
        to_mate(h, 3)
        first(h, there)
        for k in range(1, 4):
            from_mate(h, k)

    def middle(h):
        def some_rows(n, carry):
            rows = pl.ds(pl.multiple_of(n * 96, 96), 96)
            gate = gu_acc[rows, 0:FH]
            up = gu_acc[rows, FH : 2 * FH]
            sig = jax.nn.sigmoid(gate)
            act = gate * sig
            if h == 0:
                hid_s[rows, :] = (act * up).astype(BF)
                return carry
            dh = dh_acc[rows, :]
            slope = sig * (1.0 + gate * (1.0 - sig))
            dgu_s[rows, 0:FH] = (dh * up * slope).astype(BF)
            dgu_s[rows, FH : 2 * FH] = (dh * act).astype(BF)
            return carry

        lax.fori_loop(0, ROWS // 96, some_rows, 0)

    back = ((0, 1, 2, 3), (3 - y, 0, 1, 2 + y))

    def second(a, j):
        if a == 0:
            return dot(hid_s[...], dn_s[j])
        return dot_nt(dgu_s[...], gu_s[j])

    def for_mate(a, k):
        t = 4 * a + k
        xo_s[t] = second(a, far + back[a][k]).astype(BF)
        pltpu.make_async_remote_copy(
            xo_s.at[t], xi_s.at[t], xs_sem.at[t], xr_sem.at[t],
            device_id=(f, mate), device_id_type=MESH,
        ).start()

    def chip_sum(a, k):
        t = 4 * a + k
        own = second(a, base + back[a][k])
        wait_bytes(xi_s.at[t], xr_sem.at[t])
        return own + xi_s[t].astype(F32)

    def send_back(t):
        def some_rows(g, carry):
            some = v_s[pl.ds(pl.multiple_of(g * MSG, MSG), MSG), :]
            for s in range(4):
                sr_s[t, g * 4 + s] = to_message(some, s).astype(BF)
            return carry

        lax.fori_loop(0, SRC // 4, some_rows, 0)

        def one(i, carry):
            f2 = spread(i, f)
            pltpu.make_async_remote_copy(
                sr_s.at[t, f2], rr_s.at[t, f], s2_sem.at[t], r2_sem.at[t],
                device_id=(f2, crossed(f2)), device_id_type=MESH,
            ).start()
            return carry

        lax.fori_loop(1, SRC, one, 0)
        pltpu.make_async_copy(sr_s.at[t, f], rr_s.at[t, f], l2_sem.at[t]).start()

    def returned(a, k):
        v_s[...] = chip_sum(a, k)
        send_back(3 * a + k)

    def for_other():
        same = lax.rem(over_cap(iota((ROWS, W), 0)) + f, 2) == 0
        a, b = chip_sum(1, 0), chip_sum(1, 3)
        yo_s[...] = jnp.where(same, a, b).astype(BF)
        vq_s[...] = jnp.where(same, b, a)
        pltpu.make_async_remote_copy(
            yo_s, yi_s, ys_sem, yr_sem, device_id=(f, other), device_id_type=MESH
        ).start()

    def both_chips():
        wait_bytes(yi_s, yr_sem)
        v_s[...] = vq_s[...] + yi_s[...].astype(F32)
        send_back(6)

    def grads(j, carry):
        for n in range(3):
            some = slice(n * 256, (n + 1) * 256)
            gu_s[j, :, some] = dot_tn(xg_s[j, 0], dgu_s[:, some]).astype(BF)
        dn_s[j] = dot_tn(hid_s[...], xg_s[j, 1]).astype(BF)
        return carry

    def landed(t):
        wait_bytes(rr_s.at[t, pl.ds(0, SRC - 1)], r2_sem.at[t])
        pltpu.make_async_copy(sr_s.at[t, f], rr_s.at[t, f], l2_sem.at[t]).wait()

        def some_rows(g, carry):
            rows = pl.ds(pl.multiple_of(g * MSG, MSG), MSG)
            msgs = rr_s[t, pl.ds(g * 4, 4)].astype(F32)
            for q in range(4):
                u_s[t, rows, q * Q : (q + 1) * Q] = from_messages(msgs, q).astype(BF)
            return carry

        lax.fori_loop(0, SRC // 4, some_rows, 0)

    def combined(t):
        u = u_s[t]
        if t >= 4:
            return dot(et_s[...], u).astype(BF)
        return (dot(whi_s[...], u) + dot(wlo_s[...], u)).astype(BF)

    def share_partial(n):
        for k in range(2):
            landed(2 * n + k)
            po_s[n, k] = combined(2 * n + k)
        pltpu.make_async_remote_copy(
            po_s.at[n], pi_s.at[n], ps_sem.at[n], pr_sem.at[n],
            device_id=(f, other), device_id_type=MESH,
        ).start()

    def share_whole():
        n = base + 2 + y
        landed(6)
        mq_s[1, n] = combined(6)
        pltpu.make_async_remote_copy(
            mq_s.at[1, n], mq_s.at[1, n], ps_sem.at[3], pr_sem.at[3],
            device_id=(f, other), device_id_type=MESH,
        ).start()

    def hand_over(n):
        some = pl.ds(base + 2 * (n % 2), 2)
        pltpu.make_async_remote_copy(
            mq_s.at[n // 2, some], mq_s.at[n // 2, some], ms_sem.at[n], mr_sem.at[n],
            device_id=(f, mate), device_id_type=MESH,
        ).start()

    def add_partial(n):
        wait_bytes(pi_s.at[n], pr_sem.at[n])
        some = pl.ds(base + 2 * (n % 2), 2)
        mq_s[n // 2, some] = (po_s[n].astype(F32) + pi_s[n].astype(F32)).astype(BF)
        hand_over(n)

    def pass_whole():
        wait_bytes(mq_s.at[1, base + 3 - y], pr_sem.at[3])
        hand_over(3)

    def sum_route(n, device):
        copy = pltpu.make_async_remote_copy(
            dr_s.at[2 * n], dr_s.at[2 * n + 1], ds_sem.at[n], dr_sem.at[n],
            device_id=(f, device), device_id_type=MESH,
        )
        copy.start()
        return copy

    get_one(0)
    keep_two(0)
    pack_two(1)
    get_one(1)
    keep_two(1)

    gu_acc[...] = jnp.zeros_like(gu_acc)
    dh_acc[...] = jnp.zeros_like(dh_acc)
    slot_t = iota((TOK, ROWS), 1)
    owner_t = over_cap(slot_t)
    rep_t = jnp.where(owner_t == iota((TOK, ROWS), 0), 1.0, 0.0).astype(BF)
    fills_t = dot(code.T.astype(BF), rep_t) == (slot_t - CAP * owner_t + 1).astype(F32)
    et_s[...] = jnp.where(fills_t, 1.0, 0.0).astype(BF)
    wmat_t = wmat.T
    w_hi_t = wmat_t.astype(BF)
    w_lo_t = (wmat_t - w_hi_t.astype(F32)).astype(BF)
    whi_s[...] = jnp.where(fills_t, dot(w_hi_t, rep_t), 0.0).astype(BF)
    wlo_s[...] = jnp.where(fills_t, dot(w_lo_t, rep_t), 0.0).astype(BF)
    wait_bytes(gu_s, w_sem.at[0])
    wait_bytes(dn_s, w_sem.at[1])

    use_one(0)
    use_one(1)
    two_sent(0)
    to_all(send_two, 1)
    get_rest(0)
    middle(0)
    for k in range(4):
        for_mate(0, k)
    for k in range(3):
        returned(0, k)
    get_rest(1)
    middle(1)
    for k in (0, 3, 1, 2):
        for_mate(1, k)
    for_other()
    returned(0, 3)
    returned(1, 1)
    returned(1, 2)
    share_partial(0)
    both_chips()
    share_partial(1)
    lax.fori_loop(0, NP, grads, 0)
    share_partial(2)
    prod = dot_nt(dout_v[:, 0:W], u_s[0])
    for k in range(1, 4):
        prod = prod + dot_nt(dout_v[:, k * W : (k + 1) * W], u_s[k])
    kept = jnp.where(et_s[...] > 0, prod, 0.0)
    hi = kept.astype(BF)
    lo = (kept - hi.astype(F32)).astype(BF)
    group = jnp.where(over_cap(iota((ROWS, 128), 0)) == iota((ROWS, 128), 1), 1.0, 0.0).astype(BF)
    dr_s[0] = dot(hi, group) + dot(lo, group)
    route = sum_route(0, other)
    add_partial(0)
    lax.fori_loop(NP, 2 * NP, grads, 0)
    add_partial(1)
    share_whole()
    route.wait()
    dr_s[2] = dr_s[0] + dr_s[1]
    route = sum_route(1, mate)
    add_partial(2)
    route.wait()
    total = (dr_s[2] + dr_s[3]).T
    for k in range(top):
        hit = ids_s[k : k + 1, :] == expert
        droute_ref[k : k + 1, :] = jnp.sum(jnp.where(hit, total, 0.0), axis=0, keepdims=True)
    pass_whole()
    for n in range(4):
        wait_bytes(mq_s.at[n // 2, pl.ds(far + 2 * (n % 2), 2)], mr_sem.at[n])

    two_sent(1)
    for h in range(2):
        wait_bytes(xg_s.at[0, 0], qs_sem.at[h])
    for n in range(8):
        wait_bytes(xg_s.at[0, 0], fs_sem.at[n])
        wait_bytes(xo_s.at[n], xs_sem.at[n])
    for t in range(7):
        wait_bytes(sr_s.at[t, pl.ds(0, SRC - 1)], s2_sem.at[t])
    wait_bytes(yo_s, ys_sem)
    for n in range(3):
        wait_bytes(po_s.at[n], ps_sem.at[n])
    wait_bytes(mq_s.at[1, 0], ps_sem.at[3])
    for n in range(4):
        wait_bytes(mq_s.at[n // 2, pl.ds(0, 2)], ms_sem.at[n])


def store_kernel(
    mq_ref, droute_ref, gu_ref, dn_ref,
    moe_hbm, dtok_hbm, out_ref, dgate_hbm, dup_hbm, ddown_hbm, sem,
):
    copies = []
    for j in range(2 * NP):
        cols = pl.ds(j * W, W)
        copies += [
            (gu_ref.at[j, :, pl.ds(0, FH)], dgate_hbm.at[0, cols, :]),
            (gu_ref.at[j, :, pl.ds(FH, FH)], dup_hbm.at[0, cols, :]),
            (dn_ref.at[j], ddown_hbm.at[0, :, cols]),
        ]
    for a, out_hbm in enumerate((moe_hbm, dtok_hbm)):
        for n in range(2 * NP):
            copies.append((mq_ref.at[a, n], out_hbm.at[:, pl.ds(n * W, W)]))
    copies = [pltpu.make_async_copy(s, d, sem.at[n]) for n, (s, d) in enumerate(copies)]
    for one in copies:
        one.start()
    out_ref[...] = droute_ref[...]
    for one in copies:
        one.wait()


def per_device(tokens, expert_ids, route_weights, d_out, gate_weight, up_weight, down_weight):
    hbm = pl.BlockSpec(memory_space=pl.ANY)
    vmem = pl.BlockSpec(memory_space=pltpu.VMEM)
    shape = jax.ShapeDtypeStruct
    dma = pltpu.SemaphoreType.DMA
    v = pltpu.VMEM
    top = route_weights.shape[1]
    mq, droute, gu, dn = pl.pallas_call(
        kernel,
        out_shape=(
            v((2, 2 * NP, TOK, W), BF), v((top, TOK), F32),
            v((2 * NP, W, 2 * FH), BF), v((2 * NP, FH, W), BF),
        ),
        in_specs=[hbm] * 7,
        out_specs=(vmem, vmem, vmem, vmem),
        scratch_shapes=[
            v((top, TOK), jnp.int32), v((top, TOK), F32),
            v((TOK, HALF), BF), v((TOK, HALF), BF),
            v((ROWS, TOK), BF), v((ROWS, 128), F32),
            v((TOK, ROWS), BF), v((TOK, ROWS), BF), v((TOK, ROWS), BF),
            v((ROWS, 2 * W), F32),
            v((2, SRC, MSG, Q), BF), v((2, SRC, MSG, Q), BF),
            v((2, SRC, 2 * MSG, Q), BF), v((2, SRC, 2 * MSG, Q), BF),
            v((2 * NP, 2, ROWS, W), BF),
            v((ROWS, 2 * FH), F32), v((ROWS, FH), F32),
            v((ROWS, FH), BF), v((ROWS, 2 * FH), BF),
            v((8, ROWS, W), BF), v((8, ROWS, W), BF),
            v((ROWS, W), BF), v((ROWS, W), BF), v((ROWS, W), F32), v((ROWS, W), F32),
            v((7, SRC, MSG, Q), BF), v((7, SRC, MSG, Q), BF),
            v((7, ROWS, W), BF),
            v((3, 2, TOK, W), BF), v((3, 2, TOK, W), BF),
            v((4, TOK, 128), F32),
            pltpu.SemaphoreType.REGULAR((2,)),
            dma((4,)), dma((2,)), dma((4,)), dma((4,)), dma((4,)), dma((8,)), dma((8,)), dma((2,)), dma((2,)),
            dma((8,)), dma((8,)), dma, dma, dma((7,)), dma((7,)), dma((7,)),
            dma((4,)), dma((4,)), dma((4,)), dma((4,)), dma((2,)), dma((2,)),
        ],
        compiler_params=pltpu.CompilerParams(
            collective_id=0, has_side_effects=True, vmem_limit_bytes=46 * 1024 * 1024
        ),
        cost_estimate=pl.CostEstimate(flops=11_000_000_000, bytes_accessed=12_000_000, transcendentals=200_000),
    )(expert_ids.T, route_weights.T, tokens, d_out, gate_weight, up_weight, down_weight)
    moe, dtok, droute, dgate, dup, ddown = pl.pallas_call(
        store_kernel,
        out_shape=(
            shape((TOK, D), BF), shape((TOK, D), BF), shape((top, TOK), F32),
            shape(gate_weight.shape, BF), shape(up_weight.shape, BF), shape(down_weight.shape, BF),
        ),
        in_specs=[vmem, vmem, vmem, vmem],
        out_specs=(hbm, hbm, vmem, hbm, hbm, hbm),
        scratch_shapes=[dma((10 * NP,))],
        compiler_params=pltpu.CompilerParams(vmem_limit_bytes=1024 * 1024),
        cost_estimate=pl.CostEstimate(flops=0, bytes_accessed=12_000_000, transcendentals=0),
    )(mq, droute, gu, dn)
    return moe, dtok, droute.T, dgate, dup, ddown


def solution(mesh):
    in_specs = (
        P("fsdp", None),
        P("fsdp", None),
        P("fsdp", None),
        P("fsdp", None),
        P("fsdp", None, "expert"),
        P("fsdp", None, "expert"),
        P("fsdp", "expert", None),
    )
    out_specs = (
        P("fsdp", None),
        P("fsdp", None),
        P("fsdp", None),
        P("fsdp", None, "expert"),
        P("fsdp", None, "expert"),
        P("fsdp", "expert", None),
    )
    return jax.shard_map(
        per_device, mesh=mesh, in_specs=in_specs, out_specs=out_specs, check_vma=False
    )
```
